128 devices in a mesh: gx: 16 (over x, y), gy: 8 (over z, core).
Axes of the slice: x: 4, y: 4, z: 4, core: 2. Of those that a mesh axis runs over, the one named last changes fastest.
Arguments:
- level_set: float32 [16384, 8192], P('gx', 'gy'), may hold values from -6 to 6
- fuel_class: int32 [16384, 8192], P('gx', 'gy'), may hold values from 0 to 12
- ignition: int32 [2048, 1024], P('gx', 'gy'), may hold values 0 or 1
- counts: int32 [64, 32], P('gx', 'gy'), may hold values from 0 to 65536, as said below
- destination: int32 [64, 32], P('gx', 'gy'), may hold values from -1 to 15, as said below
- surface_wind: float32 [2, 2048, 1024], P(None, 'gx', 'gy'), may hold values from -9 to 9
- spread_table: float32 [13], replicated, may hold values from 0.03 to 0.25
- heat_table: float32 [13], replicated, may hold values from 1 to 8
- profile: float32 [4], replicated, may hold values from 0.2 to 1
Outputs:
- relocated: float32 [8, 256, 256, 256], P('gy', 'gx')
- heating: float32 [4, 2048, 1024], P(None, 'gx', 'gy')
The draws below stay inside these ranges and needn't reach their ends.
Inputs may be any that keep to these rules, and one draw needn't show every extreme that they name: Zero marks a spare tile. In every row of devices along gx some device has all its tiles with counts > 0. -1 exactly where counts is 0. A tile goes to a device with the same gy index as its own. For each device there is an offset o such that its k-th burning tile (numbered in row-major order of its block) has destination (k + o) mod 16; so one device hands at most 1 tiles to one device.
All inputs are finite; a program needn't handle non-finite values. No bound on the sum of `ignition` on one device may be relied on, other than what follows from the above.
Results may differ from the reference program's by a relative error of at most 0.0003.
Values sent between devices are 32-bit elements; how exact they have to be, the bound alone decides.
A program may use at most 192 MiB of HBM per device.

```python
import math
import jax
import jax.numpy as jnp
import numpy as np
from jax import lax

TILE = 256
REFINE = 8
LEV = 4
NFUEL = 13
TXD = 4
TYD = 4
NX = 2048
NY = 1024
FX = 16384
FY = 8192
N_GX = 16
N_GY = 8


def burning_plan(key):
    base = jax.random.fold_in(key, 7)
    key_level, key_pick, key_full, key_count, key_turn = jax.random.split(base, 5)
    tile_count = TXD * TYD
    level_pick = jax.random.randint(key_level, (N_GX, N_GY), 0, 11)
    threshold = level_pick * level_pick * 10
    full_device = jax.random.randint(key_full, (N_GY,), 0, N_GX)
    forced = jnp.arange(N_GX)[:, None] == full_device[None, :]
    threshold = jnp.where(forced, 1000, threshold)
    scores = jax.random.randint(key_pick, (N_GX, N_GY, tile_count), 0, 1000)
    active = scores < threshold[:, :, None]
    burning = jax.random.randint(key_count, (N_GX, N_GY, tile_count), 1, TILE * TILE + 1)
    counts = jnp.where(active, burning, 0)
    active_int = active.astype(jnp.int32)
    per_device = jnp.sum(active_int, axis=-1)
    prefix = jnp.cumsum(per_device, axis=0) - per_device
    turning = jax.random.randint(key_turn, (N_GY,), 0, N_GX)
    tile_rank = jnp.cumsum(active_int, axis=-1) - 1
    target = (prefix[:, :, None] + tile_rank + turning[None, :, None]) % N_GX
    target = jnp.where(active, target, -1)

    def layout(values):
        return values.reshape(N_GX, N_GY, TXD, TYD).transpose(0, 2, 1, 3).reshape(TXD * N_GX, TYD * N_GY).astype(jnp.int32)
    return (layout(counts), layout(target))


def draw_counts(key, part):
    return burning_plan(key)[0]


def draw_destination(key, part):
    return burning_plan(key)[1]


def with_ends(array, own_key, least, largest):
    index_at = [jax.random.randint(jax.random.fold_in(own_key, axis), (), 0, length) for axis, length in enumerate(array.shape)]
    longest = array.shape.index(max(array.shape))
    neighbour = index_at[:longest] + [(index_at[longest] + 1) % array.shape[longest]] + index_at[longest + 1:]
    return array.at[tuple(index_at)].set(least).at[tuple(neighbour)].set(largest)


def steps_of(key, dims, cuts, low, top_value):
    factor_of = 1.0
    for axis_at, blocks in cuts:
        draws = jax.random.uniform(jax.random.fold_in(jax.random.fold_in(key, 6), axis_at), (blocks,), jnp.float32, low / len(cuts), top_value / len(cuts))
        factor_of = factor_of * jnp.repeat(jnp.exp(draws), dims[axis_at] // blocks).reshape((-1,) + (1,) * (len(dims) - 1 - axis_at))
    return factor_of


def gaussian(own_key, extent, deviation, reach, shards=(), held_as=jnp.bfloat16):
    result = deviation * jax.random.normal(own_key, extent, jnp.float32)
    if shards:
        result = result * steps_of(own_key, extent, shards, -0.22, 0.18)
    return jnp.clip(result, -reach, reach).astype(held_as)


def setup_inputs(seed: int = 0) -> dict:
    key_of = jax.random.split(jax.random.key(seed), 10)
    level_set = gaussian(key_of[0], (FX, FY), 1.0, 6.0, ((0, 16), (1, 8)), jnp.float32)
    fuel_class = with_ends(jax.random.randint(key_of[1], (FX, FY), 0, NFUEL), jax.random.fold_in(key_of[1], 1), 0, NFUEL - 1).astype(jnp.int32)
    ignition = with_ends((jax.random.randint(key_of[2], (NX, NY), 0, 8) < 1).astype(jnp.int32), jax.random.fold_in(key_of[2], 1), 0, 1)
    counts = draw_counts(jax.random.fold_in(key_of[9], 71), 0)
    destination = draw_destination(jax.random.fold_in(key_of[9], 71), 0)
    surface_wind = gaussian(key_of[5], (2, NX, NY), 1.5, 9.0, ((1, 16), (2, 8)), jnp.float32)
    spread_table = jnp.clip(jnp.exp(jax.random.uniform(key_of[6], (NFUEL,), jnp.float32, math.log(0.03), math.log(0.25))), 0.03, 0.25)
    heat_table = jnp.clip(jnp.exp(jax.random.uniform(key_of[7], (NFUEL,), jnp.float32, math.log(1.0), math.log(8.0))), 1.0, 8.0)
    profile = jnp.clip(jnp.exp(jax.random.uniform(key_of[8], (LEV,), jnp.float32, math.log(0.2), math.log(1.0))), 0.2, 1.0)
    return {"level_set": level_set, "fuel_class": fuel_class, "ignition": ignition, "counts": counts, "destination": destination, "surface_wind": surface_wind, "spread_table": spread_table, "heat_table": heat_table, "profile": profile}


TIME_STEP = 0.6
IGNITE_DEPTH = 1.5
WIND_GAIN = 2.0
HIGHEST = lax.Precision.HIGHEST

def interp_table():
    coarse = TILE // REFINE
    interp = np.zeros((TILE + 4, coarse + 2), np.float32)
    for position in range(TILE + 4):
        centre = (position - 1.5) / REFINE + 0.5
        lower_cell = int(np.floor(centre))
        weight = centre - lower_cell
        interp[position, lower_cell] += 1.0 - weight
        interp[position, lower_cell + 1] += weight
    return interp

def mean_table():
    coarse = TILE // REFINE
    return np.kron(np.eye(coarse, dtype=np.float32), np.full((1, REFINE), 1.0 / REFINE, np.float32))

def advance(levels, spread, wind_x, wind_y):
    centre = levels[1:-1, 1:-1]
    back_x = centre - levels[:-2, 1:-1]
    ahead_x = levels[2:, 1:-1] - centre
    back_y = centre - levels[1:-1, :-2]
    ahead_y = levels[1:-1, 2:] - centre
    slope_x = 0.5 * (back_x + ahead_x)
    slope_y = 0.5 * (back_y + ahead_y)
    normal = jnp.sqrt(slope_x * slope_x + slope_y * slope_y + 1.0)
    tailwind = jnp.maximum((wind_x * slope_x + wind_y * slope_y) / normal, 0.0)
    spread_rate = spread * (1.0 + WIND_GAIN * tailwind * tailwind / (1.0 + tailwind * tailwind))
    upwind = jnp.sqrt(jnp.maximum(back_x, 0.0) ** 2 + jnp.minimum(ahead_x, 0.0) ** 2 + jnp.maximum(back_y, 0.0) ** 2 + jnp.minimum(ahead_y, 0.0) ** 2)
    return centre - TIME_STEP * spread_rate * upwind

def burn_tile(extended, spread_ext, heat_tile, wind_tile):
    interp = jnp.asarray(interp_table(), jnp.float32)
    averaging = jnp.asarray(mean_table(), jnp.float32)

    def to_fire(field):
        inner_product = jnp.dot(interp, field, precision=HIGHEST, preferred_element_type=jnp.float32)
        return jnp.dot(inner_product, interp.T, precision=HIGHEST, preferred_element_type=jnp.float32)
    wind_x = to_fire(wind_tile[0])
    wind_y = to_fire(wind_tile[1])
    halfway = advance(extended, spread_ext[1:-1, 1:-1], wind_x[1:-1, 1:-1], wind_y[1:-1, 1:-1])
    second = advance(halfway, spread_ext[2:-2, 2:-2], wind_x[2:-2, 2:-2], wind_y[2:-2, 2:-2])
    burned_before = jnp.clip(0.5 - extended[2:-2, 2:-2], 0.0, 1.0)
    burned_after = jnp.clip(0.5 - second, 0.0, 1.0)
    release = heat_tile * (burned_after - burned_before) / (2.0 * TIME_STEP)
    partial_mean = jnp.dot(averaging, release, precision=HIGHEST, preferred_element_type=jnp.float32)
    tile_flux = jnp.dot(partial_mean, averaging.T, precision=HIGHEST, preferred_element_type=jnp.float32)
    return (second, tile_flux)

def reference(level_set, fuel_class, ignition, counts, destination, surface_wind, spread_table, heat_table, profile):
    coarse = TILE // REFINE
    tiles_x = TXD * N_GX
    tiles_y = TYD * N_GY
    ignite = jnp.repeat(jnp.repeat(ignition.astype(jnp.float32), REFINE, 0), REFINE, 1)
    ignited = level_set - IGNITE_DEPTH * ignite
    spread = jnp.take(spread_table, fuel_class)
    heat_field = jnp.take(heat_table, fuel_class)
    padded = jnp.pad(jnp.stack([ignited, spread]), ((0, 0), (2, 2), (2, 2)))
    wind_pad = jnp.pad(surface_wind, ((0, 0), (1, 1), (1, 1)))

    def one_row(index_x):

        def one_tile(index_y):
            extended = lax.dynamic_slice(padded, (jnp.int32(0), index_x * TILE, index_y * TILE), (2, TILE + 4, TILE + 4))
            heat_tile = lax.dynamic_slice(heat_field, (index_x * TILE, index_y * TILE), (TILE, TILE))
            wind_tile = lax.dynamic_slice(wind_pad, (jnp.int32(0), index_x * coarse, index_y * coarse), (2, coarse + 2, coarse + 2))
            return burn_tile(extended[0], extended[1], heat_tile, wind_tile)
        return jax.vmap(one_tile)(jnp.arange(tiles_y, dtype=jnp.int32))
    updated, fluxes = lax.map(one_row, jnp.arange(tiles_x, dtype=jnp.int32))
    active = counts > 0
    fluxes = jnp.where(active[:, :, None, None], fluxes, 0.0)
    flux_grid = fluxes.transpose(0, 2, 1, 3).reshape(tiles_x * coarse, tiles_y * coarse)
    heating = profile[:, None, None] * flux_grid[None]
    blocks = active.astype(jnp.int32).reshape(N_GX, TXD, N_GY, TYD).transpose(0, 2, 1, 3).reshape(N_GX, N_GY, TXD * TYD)
    tile_rank = jnp.cumsum(blocks, axis=-1) - 1
    tile_rank = tile_rank.reshape(N_GX, N_GY, TXD, TYD).transpose(0, 2, 1, 3).reshape(tiles_x, tiles_y)
    capacity = (TXD * TYD + N_GX - 1) // N_GX
    slot_count = capacity * N_GX
    source = (jnp.arange(tiles_x, dtype=jnp.int32) // TXD)[:, None]
    row_index = jnp.broadcast_to((jnp.arange(tiles_y, dtype=jnp.int32) // TYD)[None, :], (tiles_x, tiles_y))
    column = destination * slot_count + source * capacity + tile_rank // N_GX
    column = jnp.where(active, column, N_GX * slot_count).astype(jnp.int32)
    relocated = jnp.zeros((N_GY, N_GX * slot_count, TILE, TILE), jnp.float32)
    relocated = relocated.at[row_index, column].set(updated, mode='drop')
    return (relocated, heating)
```

```python
import jax
import jax.numpy as jnp
from jax import lax
from jax.experimental import pallas as pl
from jax.experimental.pallas import tpu as pltpu
from jax.sharding import PartitionSpec as P

TILE = 256
REFINE = 8
NFUEL = 13
LEV = 4
TIME_STEP = 0.6
IGNITE_DEPTH = 1.5
N_GX = 16
N_GY = 8
SIDE = 1024
COARSE = 128
RING = 384
TINY = 1e-30
MESH = pl.DeviceIdType.MESH
F32 = jnp.float32
BF16 = jnp.bfloat16

OFFSETS = (
    (2, 2), (2, 1), (1, 2), (2, 3), (3, 2), (1, 1), (3, 3), (1, 3),
    (3, 1), (2, 0), (0, 2), (1, 0), (0, 1), (3, 0), (0, 3), (0, 0),
)


def split(x):
    high = x.astype(BF16)
    return high, (x - high.astype(F32)).astype(BF16)


def dot2(a, b):
    high, low = split(a)
    return jnp.dot(high, b, preferred_element_type=F32) + jnp.dot(
        low, b, preferred_element_type=F32
    )


def advance(centre, up, down, left, right, wind_x, wind_y, reach):
    back_x = centre - up
    ahead_x = down - centre
    back_y = centre - left
    ahead_y = right - centre
    twice_x = down - up
    twice_y = right - left
    push = jnp.maximum(wind_x * twice_x + wind_y * twice_y, 0.0)
    push2 = push * push
    whole = twice_x * twice_x + twice_y * twice_y + 4.0 + push2
    gain = whole + 2.0 * push2
    px = jnp.maximum(back_x, 0.0)
    nx = jnp.minimum(ahead_x, 0.0)
    py = jnp.maximum(back_y, 0.0)
    ny = jnp.minimum(ahead_y, 0.0)
    upwind2 = (px * px + nx * nx) + (py * py + ny * ny)
    scale = lax.rsqrt(jnp.maximum(upwind2, TINY) * (whole * whole))
    return centre - (reach * gain) * (upwind2 * scale)


def lookup(table, scale, codes):
    values = [table[t] * scale for t in range(NFUEL)]
    bit = 1
    while len(values) > 1:
        odd = (codes & bit) != 0
        values = [
            jnp.where(odd, values[t + 1], values[t]) if t + 1 < len(values) else values[t]
            for t in range(0, len(values), 2)
        ]
        bit *= 2
    return values[0]


def kernel(
    level_hbm, fuel_hbm, ignition_hbm, wind_hbm, spread_hbm, heat_hbm, plan_hbm, profile_hbm,
    out, heating,
    levels, spreads, fuels, winds, level, spread, heat, halfway, fire_wind,
    ignition, wind, spread_table, heat_table, plan, profile,
    wind_pad, row_weight, ignite, stage, release, flux,
    row_send, row_recv, col_send, col_recv, diag_send, diag_recv,
    small_sem, level_sem, fuel_sem,
    row_sem, col_sem, diag_sem, row_rsem, col_rsem, diag_rsem, send_sem, recv_sem, own_sem,
):
    gx = lax.axis_index("gx")
    gy = lax.axis_index("gy")
    my_x = gx // 4
    my_y = gx % 4
    gx_at = ((gx + N_GX - 1) % N_GX, (gx + 1) % N_GX)
    gy_at = ((gy + N_GY - 1) % N_GY, (gy + 1) % N_GY)

    small = [
        pltpu.make_async_copy(source, here, small_sem.at[n])
        for n, (source, here) in enumerate((
            (ignition_hbm, ignition), (spread_hbm, spread_table), (wind_hbm, wind),
            (heat_hbm, heat_table), (plan_hbm, plan), (profile_hbm, profile),
        ))
    ]
    for copy in small:
        copy.start()
    loads = []
    for k in range(16):
        block = (pl.ds(k // 4 * TILE, TILE), pl.ds(k % 4 * TILE, TILE))
        loads.append(
            pltpu.make_async_copy(
                level_hbm.at[block], levels.at[k, pl.ds(8, TILE), pl.ds(0, TILE)], level_sem.at[k]
            )
        )
        loads.append(pltpu.make_async_copy(fuel_hbm.at[block], fuels.at[k], fuel_sem.at[k]))
    for copy in loads:
        copy.start()

    barrier = pltpu.get_barrier_semaphore()
    for ox, oy in OFFSETS[:-1]:
        peer = ((my_x + ox) % 4) * 4 + (my_y + oy) % 4
        pl.semaphore_signal(
            barrier, inc=1, device_id={"gx": peer, "gy": gy}, device_id_type=MESH
        )
    for b in range(2):
        for px in (gx, gx_at[0], gx_at[1]):
            pl.semaphore_signal(
                barrier, inc=1, device_id={"gx": px, "gy": gy_at[b]}, device_id_type=MESH
            )

    lane = lax.broadcasted_iota(jnp.int32, (1, 128), 1)
    low_lane = lane < 64

    levels[16] = jnp.zeros((TILE + 16, RING), F32)
    spreads[16] = jnp.zeros((TILE + 16, RING), F32)
    fuels[16] = jnp.zeros((TILE, TILE), jnp.int32)
    winds[16] = jnp.zeros((96, 2 * RING), BF16)
    flux[16] = jnp.zeros((32, 128), F32)

    fire_row = (lax.broadcasted_iota(jnp.int32, (TILE + 16, 96), 0) - 8).astype(F32)
    coarse_row = lax.broadcasted_iota(jnp.int32, (TILE + 16, 96), 1)
    coarse_row = (jnp.where(coarse_row >= 48, coarse_row - 48, coarse_row) - 8).astype(F32)
    tent = 1.0 - jnp.abs((fire_row + 0.5) * (1.0 / REFINE) - 0.5 - coarse_row)
    row_weight[...] = jnp.maximum(tent, 0.0).astype(BF16)

    for copy in small:
        copy.wait()
    cell = lax.broadcasted_iota(jnp.int32, (COARSE, TILE), 0)
    at = lax.broadcasted_iota(jnp.int32, (COARSE, TILE), 1) // REFINE
    burning = ignition[...].astype(F32).astype(BF16)
    for t in range(4):
        repeat = jnp.where(cell == at + t * 32, IGNITE_DEPTH, 0.0).astype(BF16)
        ignite[t] = jnp.dot(burning, repeat, preferred_element_type=F32)

    def prepare(tile_x, tile_y, block, subs, halves):
        k = tile_x * 4 + tile_y
        for half in halves:
            lanes = pl.ds(half * 128, 128)
            burned = ignite[tile_y, pl.ds(pl.multiple_of(tile_x * 32 + block * 8, 8), 8), lanes]
            for s in subs:
                inner = pl.ds(pl.multiple_of(block * 64 + s * 8 + 8, 8), 8)
                levels[k, inner, lanes] = levels[k, inner, lanes] - burned[s : s + 1, :]
                codes = fuels[k, pl.ds(pl.multiple_of(block * 64 + s * 8, 8), 8), lanes]
                spreads[k, inner, lanes] = lookup(spread_table, TIME_STEP, codes)

    for copy in loads:
        copy.wait()

    def prepare_edges(block, carry):
        prepare(block // 4, 0, block % 4, range(8), (0,))
        prepare(block // 4, 3, block % 4, range(8), (1,))
        return carry

    lax.fori_loop(0, 16, prepare_edges, 0)
    for tile_y, halves in ((0, (1,)), (1, (0, 1)), (2, (0, 1)), (3, (0,))):
        prepare(0, tile_y, 0, (0,), halves)
        prepare(3, tile_y, 3, (7,), halves)

    wind_edges = (0, COARSE - 8)
    for b in range(2):
        rows = pl.ds(b * (TILE - 8) + 8, 8)
        for t in range(4):
            lanes = pl.ds(t * TILE, TILE)
            row_send[b, 0:8, lanes] = levels[b * 12 + t, rows, 0:TILE]
            row_send[b, 8:16, lanes] = spreads[b * 12 + t, rows, 0:TILE]
        for c in range(2):
            row_send[b, c * 8 : c * 8 + 8, SIDE : SIDE + 128] = wind[c, pl.ds(wind_edges[b], 8), :]
        for a in range(2):
            diag_send[b * 2 + a, 0:8, :] = levels[b * 12 + a * 3, rows, pl.ds(a * 128, 128)]
            for c in range(2):
                diag_send[b * 2 + a, 8 + c * 8 : 16 + c * 8, :] = wind[c, pl.ds(wind_edges[b], 8), :]
    for a in range(2):
        source = pl.ds(a * 128, 128)
        packed = jnp.zeros((32, 128), F32)
        for g in range(32):
            k = g // 8 * 4 + a * 3
            rows = pl.ds(8 + g % 8 * 32, 32)
            to_level = (4 * g + 2 - (126 if a else 0)) % 128
            to_spread = (4 * g + 1 - (127 if a else 0)) % 128
            moved = jnp.where(
                lane % 4 == 1,
                pltpu.roll(spreads[k, rows, source], to_spread, 1),
                pltpu.roll(levels[k, rows, source], to_level, 1),
            )
            if g < 8:
                to_wind = (4 * g - (127 if a else 0)) % 128
                moved = jnp.where(
                    lane % 4 == 0,
                    pltpu.roll(wind[g // 4, pl.ds((g % 4) * 32, 32), :], to_wind, 1),
                    moved,
                )
            packed = jnp.where(lane // 4 == g, moved, packed)
        col_send[a] = packed

    pl.semaphore_wait(barrier, len(OFFSETS) - 1 + 6)

    halos = []
    for b in range(2):
        halos.append(
            pltpu.make_async_remote_copy(
                src_ref=row_send.at[b], dst_ref=row_recv.at[1 - b],
                send_sem=row_sem.at[b], recv_sem=row_rsem.at[1 - b],
                device_id={"gx": gx_at[b], "gy": gy}, device_id_type=MESH,
            )
        )
        halos.append(
            pltpu.make_async_remote_copy(
                src_ref=col_send.at[b], dst_ref=col_recv.at[1 - b],
                send_sem=col_sem.at[b], recv_sem=col_rsem.at[1 - b],
                device_id={"gx": gx, "gy": gy_at[b]}, device_id_type=MESH,
            )
        )
        for a in range(2):
            k = b * 2 + a
            halos.append(
                pltpu.make_async_remote_copy(
                    src_ref=diag_send.at[k], dst_ref=diag_recv.at[3 - k],
                    send_sem=diag_sem.at[k], recv_sem=diag_rsem.at[3 - k],
                    device_id={"gx": gx_at[b], "gy": gy_at[a]}, device_id_type=MESH,
                )
            )
    for copy in halos:
        copy.start()

    def prepare_rest(block, carry):
        for tile_y, halves in ((0, (1,)), (1, (0, 1)), (2, (0, 1)), (3, (0,))):
            prepare(block // 4, tile_y, block % 4, range(8), halves)
        return carry

    for tile_y, halves in ((0, (1,)), (1, (0, 1)), (2, (0, 1)), (3, (0,))):
        prepare(0, tile_y, 0, range(1, 8), halves)
        prepare(3, tile_y, 3, range(7), halves)
    lax.fori_loop(1, 15, prepare_rest, 0)

    edge_lanes = pl.ds(TILE, 128)

    def set_edges(block, carry):
        rows = pl.ds(pl.multiple_of(block % 4 * 64 + 8, 8), 64)
        k = block // 4 * 4
        for ref in (levels, spreads):
            ref[k, rows, edge_lanes] = ref[k + 1, rows, 0:128]
            for t in (1, 2):
                ref[k + t, rows, edge_lanes] = jnp.where(
                    low_lane, ref[k + t + 1, rows, 0:128], ref[k + t - 1, rows, 128:256]
                )
            ref[k + 3, rows, edge_lanes] = ref[k + 2, rows, 128:256]
        return carry

    lax.fori_loop(0, 16, set_edges, 0)

    for c in range(2):
        wind_pad[c, 8 : 8 + COARSE, 0:128] = wind[c]

    column = lax.broadcasted_iota(jnp.int32, (256, RING), 0)
    column = jnp.where(column >= 192, column - 256, column)
    fire = lax.broadcasted_iota(jnp.int32, (256, RING), 1)
    fire = jnp.where(fire >= 320, fire - RING, fire)
    offset = (fire.astype(F32) + 0.5) * (1.0 / REFINE) - 0.5 - column.astype(F32)

    has_row = (gx > 0, gx < N_GX - 1)
    has_col = (gy > 0, gy < N_GY - 1)

    for copy in halos:
        copy.wait()

    cols = [jnp.where(has_col[a], col_recv[a], 0.0) for a in range(2)]
    for g in range(32):
        rows = pl.ds(8 + g % 8 * 32, 32)
        for ref, item, last in ((levels, 2, 126), (spreads, 1, 127)):
            k = g // 8 * 4
            got = pltpu.roll(cols[0], (last - (4 * g + item)) % 128, 1)
            ref[k, rows, edge_lanes] = jnp.where(low_lane, ref[k, rows, edge_lanes], got)
            got = pltpu.roll(cols[1], (0 - (4 * g + item)) % 128, 1)
            ref[k + 3, rows, edge_lanes] = jnp.where(low_lane, got, ref[k + 3, rows, edge_lanes])
        if g < 8:
            ends = [pltpu.roll(cols[a], ((0 if a else 127) - 4 * g) % 128, 1) for a in range(2)]
            wind_pad[g // 4, pl.ds(8 + (g % 4) * 32, 32), 128:256] = jnp.where(
                low_lane, ends[1], ends[0]
            )
    for b in range(2):
        rows = pl.ds(b * (TILE + 8), 8)
        from_rows = pl.ds(8 if b else TILE, 8)
        for k in range(16):
            if k // 4 == b * 3:
                t = k % 4
                for ref, part in ((levels, 0), (spreads, 8)):
                    got = row_recv[b, part : part + 8, :]
                    ref[k, rows, 0:TILE] = jnp.where(has_row[b], got[:, t * TILE : t * TILE + TILE], 0.0)
                    corner = [
                        jnp.where(has_col[a], diag_recv[b * 2 + a, 0:8, :], 0.0) for a in range(2)
                    ]
                    last = corner[0] if t == 0 else got[:, t * TILE - 128 : t * TILE]
                    after = corner[1] if t == 3 else got[:, t * TILE + TILE : t * TILE + TILE + 128]
                    ref[k, rows, edge_lanes] = jnp.where(
                        has_row[b], jnp.where(low_lane, after, last), 0.0
                    )
            else:
                for ref in (levels, spreads):
                    ref[k, rows, :] = ref[k + (4 if b else -4), from_rows, :]
        wind_at = pl.ds(b * (COARSE + 8), 8)
        for c in range(2):
            wind_pad[c, wind_at, 0:128] = jnp.where(
                has_row[b], row_recv[b, c * 8 : c * 8 + 8, SIDE : SIDE + 128], 0.0
            )
            ends = [
                jnp.where(has_col[a], diag_recv[b * 2 + a, 8 + c * 8 : 16 + c * 8, :], 0.0)
                for a in range(2)
            ]
            wind_pad[c, wind_at, 128:256] = jnp.where(
                has_row[b], jnp.where(low_lane, ends[1], ends[0]), 0.0
            )

    for t in range(4):
        weight = jnp.maximum(1.0 - jnp.abs(offset + 32.0 * t), 0.0).astype(BF16)
        for c in range(2):
            high, low = split(dot2(wind_pad[c], weight))
            for tx in range(4):
                lanes = pl.ds(c * RING, RING)
                winds[tx * 4 + t, 0:48, lanes] = high[tx * 32 : tx * 32 + 48]
                winds[tx * 4 + t, 48:96, lanes] = low[tx * 32 : tx * 32 + 48]

    sub = lax.broadcasted_iota(jnp.int32, (8, RING), 0)
    sub_in = lax.broadcasted_iota(jnp.int32, (8, TILE), 0)
    place = jnp.where(
        lax.broadcasted_iota(jnp.int32, (TILE, 128), 0) // REFINE
        == lax.broadcasted_iota(jnp.int32, (TILE, 128), 1),
        1.0,
        0.0,
    ).astype(BF16)

    def eight(i):
        return pl.ds(pl.multiple_of(i * 8, 8), 8)

    def one_tile(j, carry):
        ox = jnp.int32(0)
        oy = jnp.int32(0)
        for i, (dx, dy) in enumerate(OFFSETS):
            now = (j == i).astype(jnp.int32)
            ox = ox + now * dx
            oy = oy + now * dy
        target = ((my_x + ox) % 4) * 4 + (my_y + oy) % 4

        chosen = plan[target]
        level[0 : TILE + 16, :] = levels[chosen]
        spread[...] = spreads[chosen]
        heat[...] = lookup(heat_table, 1.0 / (2.0 * TIME_STEP * REFINE * REFINE), fuels[chosen])
        fire_wind[...] = jnp.dot(row_weight[...], winds[chosen], preferred_element_type=F32)

        def first(i, carry):
            above, centre = carry
            below = level[eight(i + 1), :]
            up = pltpu.roll(jnp.where(sub == 7, above, centre), 1, 0)
            down = pltpu.roll(jnp.where(sub == 0, below, centre), 7, 0)
            left = pltpu.roll(centre, 1, 1)
            right = pltpu.roll(centre, RING - 1, 1)
            halfway[eight(i), :] = advance(
                centre, up, down, left, right,
                fire_wind[eight(i), 0:RING], fire_wind[eight(i), RING : 2 * RING],
                spread[eight(i), :],
            )
            return centre, below

        level[TILE + 16 :, :] = level[TILE + 8 : TILE + 16, :]
        lax.fori_loop(0, TILE // 8 + 2, first, (level[0:8, :], level[0:8, :]), unroll=2)

        def second(i, carry):
            above, centre = carry
            below = halfway[eight(i + 2), :]
            inner = centre[:, 0:TILE]
            up = pltpu.roll(jnp.where(sub_in == 7, above[:, 0:TILE], inner), 1, 0)
            down = pltpu.roll(jnp.where(sub_in == 0, below[:, 0:TILE], inner), 7, 0)
            left = pltpu.roll(centre, 1, 1)[:, 0:TILE]
            right = pltpu.roll(centre, RING - 1, 1)[:, 0:TILE]
            result = advance(
                inner, up, down, left, right,
                fire_wind[eight(i + 1), 0:TILE], fire_wind[eight(i + 1), RING : RING + TILE],
                spread[eight(i + 1), 0:TILE],
            )
            before = jnp.clip(0.5 - level[eight(i + 1), 0:TILE], 0.0, 1.0)
            after = jnp.clip(0.5 - result, 0.0, 1.0)
            released = heat[eight(i), :] * (after - before)
            release[0, eight(i), :] = released[:, 0:128]
            release[1, eight(i), :] = released[:, 128:256]
            stage[target, eight(i), :] = result
            return centre, below

        lax.fori_loop(0, TILE // 8, second, (halfway[0:8, :], halfway[8:16, :]), unroll=2)

        @pl.when(j < len(OFFSETS) - 1)
        def _():
            pltpu.make_async_remote_copy(
                src_ref=stage.at[target], dst_ref=out.at[gx],
                send_sem=send_sem.at[j], recv_sem=recv_sem.at[j],
                device_id={"gx": target, "gy": gy}, device_id_type=MESH,
            ).start()

        rows = []
        for half in range(2):
            total = release[half, pl.ds(0, 32, stride=8), :]
            for s in range(1, 8):
                total = total + release[half, pl.ds(s, 32, stride=8), :]
            rows.append(total)
        flux[target] = dot2(jnp.concatenate(rows, axis=1), place)
        return carry

    lax.fori_loop(0, len(OFFSETS), one_tile, 0)

    own = pltpu.make_async_copy(stage.at[gx], out.at[gx], own_sem)
    own.start()

    for tx in range(4):
        band = jnp.zeros((32, 128), F32)
        for ty in range(4):
            band = band + pltpu.roll(flux[plan[16 + tx * 4 + ty]], ty * 32, 1)
        for l in range(LEV):
            heating[l, tx * 32 : tx * 32 + 32, :] = profile[l] * band

    own.wait()

    def finish(j, carry):
        pltpu.make_async_remote_copy(
            src_ref=stage.at[gx], dst_ref=out.at[gx],
            send_sem=send_sem.at[j], recv_sem=recv_sem.at[j],
            device_id={"gx": (gx + 1) % N_GX, "gy": gy}, device_id_type=MESH,
        ).wait()
        return carry

    lax.fori_loop(0, len(OFFSETS) - 1, finish, 0)


def body(
    level_set, fuel_class, ignition, counts, destination, surface_wind, spread_table, heat_table, profile
):
    hbm = pl.BlockSpec(memory_space=pltpu.HBM)
    vmem = pl.BlockSpec(memory_space=pltpu.VMEM)
    dma = pltpu.SemaphoreType.DMA

    target = jnp.where(counts > 0, destination, 16).reshape(16)
    ids = jnp.arange(16, dtype=jnp.int32)
    taken = jnp.min(jnp.where(target[None, :] == ids[:, None], ids[None, :], 16), axis=1)
    plan = jnp.concatenate([taken, target])

    relocated, heating = pl.pallas_call(
        kernel,
        out_shape=(
            jax.ShapeDtypeStruct((N_GX, TILE, TILE), F32),
            jax.ShapeDtypeStruct((LEV, COARSE, COARSE), F32),
        ),
        in_specs=[hbm] * 8,
        out_specs=(vmem, vmem),
        scratch_shapes=[
            pltpu.VMEM((17, TILE + 16, RING), F32),
            pltpu.VMEM((17, TILE + 16, RING), F32),
            pltpu.VMEM((17, TILE, TILE), jnp.int32),
            pltpu.VMEM((17, 96, 2 * RING), BF16),
            pltpu.VMEM((TILE + 24, RING), F32),
            pltpu.VMEM((TILE + 16, RING), F32),
            pltpu.VMEM((TILE, TILE), F32),
            pltpu.VMEM((TILE + 16, RING), F32),
            pltpu.VMEM((TILE + 16, 2 * RING), F32),
            pltpu.VMEM((COARSE, COARSE), jnp.int32),
            pltpu.VMEM((2, COARSE, COARSE), F32),
            pltpu.SMEM((NFUEL,), F32),
            pltpu.SMEM((NFUEL,), F32),
            pltpu.SMEM((32,), jnp.int32),
            pltpu.SMEM((LEV,), F32),
            pltpu.VMEM((2, COARSE + 16, 256), F32),
            pltpu.VMEM((TILE + 16, 96), BF16),
            pltpu.VMEM((4, COARSE, TILE), F32),
            pltpu.VMEM((N_GX, TILE, TILE), F32),
            pltpu.VMEM((2, TILE, 128), F32),
            pltpu.VMEM((17, 32, 128), F32),
            pltpu.VMEM((2, 16, SIDE + 128), F32),
            pltpu.VMEM((2, 16, SIDE + 128), F32),
            pltpu.VMEM((2, 32, 128), F32),
            pltpu.VMEM((2, 32, 128), F32),
            pltpu.VMEM((4, 24, 128), F32),
            pltpu.VMEM((4, 24, 128), F32),
            dma((6,)),
            dma((16,)),
            dma((16,)),
            dma((2,)),
            dma((2,)),
            dma((4,)),
            dma((2,)),
            dma((2,)),
            dma((4,)),
            dma((16,)),
            dma((16,)),
            dma,
        ],
        compiler_params=pltpu.CompilerParams(
            collective_id=0, has_side_effects=True, vmem_limit_bytes=44 << 20
        ),
    )(
        level_set, fuel_class, ignition, surface_wind, spread_table, heat_table, plan, profile
    )
    return relocated.reshape(1, N_GX, TILE, TILE), heating


def solution(mesh):
    in_specs = (
        P("gx", "gy"),
        P("gx", "gy"),
        P("gx", "gy"),
        P("gx", "gy"),
        P("gx", "gy"),
        P(None, "gx", "gy"),
        P(),
        P(),
        P(),
    )
    out_specs = (P("gy", "gx", None, None), P(None, "gx", "gy"))
    return jax.shard_map(body, mesh=mesh, in_specs=in_specs, out_specs=out_specs, check_vma=False)
```

```python
import jax
import jax.numpy as jnp
from jax import lax
from jax.experimental import pallas as pl
from jax.experimental.pallas import tpu as pltpu
from jax.sharding import PartitionSpec as P

TILE = 256
REFINE = 8
NFUEL = 13
LEV = 4
TIME_STEP = 0.6
IGNITE_DEPTH = 1.5
N_GX = 16
N_GY = 8
SIDE = 1024
COARSE = 128
RING = 384
TINY = 1e-30
PARTS = 4
PART = TILE // PARTS
GROUPS = PART // 8
MESH = pl.DeviceIdType.MESH
F32 = jnp.float32
BF16 = jnp.bfloat16

OFFSETS = (
    (2, 2), (2, 1), (1, 2), (2, 3), (3, 2), (1, 1), (3, 3), (1, 3),
    (3, 1), (2, 0), (0, 2), (1, 0), (0, 1), (3, 0), (0, 3), (0, 0),
)


def split(x):
    high = x.astype(BF16)
    return high, (x - high.astype(F32)).astype(BF16)


def dot2(a, b):
    high, low = split(a)
    return jnp.dot(high, b, preferred_element_type=F32) + jnp.dot(
        low, b, preferred_element_type=F32
    )


def advance(centre, up, down, left, right, wind_x, wind_y, reach):
    back_x = centre - up
    ahead_x = down - centre
    back_y = centre - left
    ahead_y = right - centre
    twice_x = down - up
    twice_y = right - left
    push = jnp.maximum(wind_x * twice_x + wind_y * twice_y, 0.0)
    push2 = push * push
    whole = twice_x * twice_x + twice_y * twice_y + 4.0 + push2
    gain = whole + 2.0 * push2
    px = jnp.maximum(back_x, 0.0)
    nx = jnp.minimum(ahead_x, 0.0)
    py = jnp.maximum(back_y, 0.0)
    ny = jnp.minimum(ahead_y, 0.0)
    upwind2 = (px * px + nx * nx) + (py * py + ny * ny)
    scale = lax.rsqrt(jnp.maximum(upwind2, TINY) * (whole * whole))
    return centre - (reach * gain) * (upwind2 * scale)


def lookup(table, scale, codes):
    values = [table[t] * scale for t in range(NFUEL)]
    bit = 1
    while len(values) > 1:
        odd = (codes & bit) != 0
        values = [
            jnp.where(odd, values[t + 1], values[t]) if t + 1 < len(values) else values[t]
            for t in range(0, len(values), 2)
        ]
        bit *= 2
    return values[0]


def kernel(
    level_hbm, fuel_hbm, ignition_hbm, wind_hbm, spread_hbm, heat_hbm, plan_hbm, profile_hbm,
    out, heating,
    levels, spreads, fuels, winds, halfway, fire_wind,
    ignition, wind, spread_table, heat_table, plan, profile,
    wind_pad, row_weight, ignite, stage, release, flux,
    row_send, row_recv, col_send, col_recv, diag_send, diag_recv,
    small_sem, level_sem, fuel_sem,
    row_sem, col_sem, diag_sem, row_rsem, col_rsem, diag_rsem, send_sem, recv_sem, own_sem,
):
    gx = lax.axis_index("gx")
    gy = lax.axis_index("gy")
    my_x = gx // 4
    my_y = gx % 4
    gx_at = ((gx + N_GX - 1) % N_GX, (gx + 1) % N_GX)
    gy_at = ((gy + N_GY - 1) % N_GY, (gy + 1) % N_GY)

    small = [
        pltpu.make_async_copy(source, here, small_sem.at[n])
        for n, (source, here) in enumerate((
            (ignition_hbm, ignition), (spread_hbm, spread_table), (wind_hbm, wind),
            (heat_hbm, heat_table), (plan_hbm, plan), (profile_hbm, profile),
        ))
    ]
    for copy in small:
        copy.start()
    loads = []
    for k in range(16):
        block = (pl.ds(k // 4 * TILE, TILE), pl.ds(k % 4 * TILE, TILE))
        loads.append(
            pltpu.make_async_copy(
                level_hbm.at[block], levels.at[k, pl.ds(8, TILE), pl.ds(0, TILE)], level_sem.at[k]
            )
        )
        loads.append(pltpu.make_async_copy(fuel_hbm.at[block], fuels.at[k], fuel_sem.at[k]))
    for copy in loads:
        copy.start()

    barrier = pltpu.get_barrier_semaphore()
    for ox, oy in OFFSETS[:-1]:
        peer = ((my_x + ox) % 4) * 4 + (my_y + oy) % 4
        pl.semaphore_signal(
            barrier, inc=1, device_id={"gx": peer, "gy": gy}, device_id_type=MESH
        )
    for b in range(2):
        for px in (gx, gx_at[0], gx_at[1]):
            pl.semaphore_signal(
                barrier, inc=1, device_id={"gx": px, "gy": gy_at[b]}, device_id_type=MESH
            )

    lane = lax.broadcasted_iota(jnp.int32, (1, 128), 1)
    low_lane = lane < 64

    levels[16] = jnp.zeros((TILE + 16, RING), F32)
    spreads[16] = jnp.zeros((TILE + 16, RING), F32)
    fuels[16] = jnp.zeros((TILE, TILE), jnp.int32)
    winds[16] = jnp.zeros((96, 2 * RING), BF16)
    flux[16] = jnp.zeros((32, 128), F32)

    fire_row = (lax.broadcasted_iota(jnp.int32, (TILE + 16, 96), 0) - 8).astype(F32)
    coarse_row = lax.broadcasted_iota(jnp.int32, (TILE + 16, 96), 1)
    coarse_row = (jnp.where(coarse_row >= 48, coarse_row - 48, coarse_row) - 8).astype(F32)
    tent = 1.0 - jnp.abs((fire_row + 0.5) * (1.0 / REFINE) - 0.5 - coarse_row)
    row_weight[...] = jnp.maximum(tent, 0.0).astype(BF16)

    for copy in small:
        copy.wait()
    cell = lax.broadcasted_iota(jnp.int32, (COARSE, TILE), 0)
    at = lax.broadcasted_iota(jnp.int32, (COARSE, TILE), 1) // REFINE
    burning = ignition[...].astype(F32).astype(BF16)
    for t in range(4):
        repeat = jnp.where(cell == at + t * 32, IGNITE_DEPTH, 0.0).astype(BF16)
        ignite[t] = jnp.dot(burning, repeat, preferred_element_type=F32)

    def prepare(tile_x, tile_y, block, subs, halves):
        k = tile_x * 4 + tile_y
        for half in halves:
            lanes = pl.ds(half * 128, 128)
            burned = ignite[tile_y, pl.ds(pl.multiple_of(tile_x * 32 + block * 8, 8), 8), lanes]
            for s in subs:
                inner = pl.ds(pl.multiple_of(block * 64 + s * 8 + 8, 8), 8)
                levels[k, inner, lanes] = levels[k, inner, lanes] - burned[s : s + 1, :]
                codes = fuels[k, pl.ds(pl.multiple_of(block * 64 + s * 8, 8), 8), lanes]
                spreads[k, inner, lanes] = lookup(spread_table, TIME_STEP, codes)

    for copy in loads:
        copy.wait()

    def prepare_edges(block, carry):
        prepare(block // 4, 0, block % 4, range(8), (0,))
        prepare(block // 4, 3, block % 4, range(8), (1,))
        return carry

    lax.fori_loop(0, 16, prepare_edges, 0)
    for tile_y, halves in ((0, (1,)), (1, (0, 1)), (2, (0, 1)), (3, (0,))):
        prepare(0, tile_y, 0, (0,), halves)
        prepare(3, tile_y, 3, (7,), halves)

    wind_edges = (0, COARSE - 8)
    for b in range(2):
        rows = pl.ds(b * (TILE - 8) + 8, 8)
        for t in range(4):
            lanes = pl.ds(t * TILE, TILE)
            row_send[b, 0:8, lanes] = levels[b * 12 + t, rows, 0:TILE]
            row_send[b, 8:16, lanes] = spreads[b * 12 + t, rows, 0:TILE]
        for c in range(2):
            row_send[b, c * 8 : c * 8 + 8, SIDE : SIDE + 128] = wind[c, pl.ds(wind_edges[b], 8), :]
        for a in range(2):
            diag_send[b * 2 + a, 0:8, :] = levels[b * 12 + a * 3, rows, pl.ds(a * 128, 128)]
            for c in range(2):
                diag_send[b * 2 + a, 8 + c * 8 : 16 + c * 8, :] = wind[c, pl.ds(wind_edges[b], 8), :]
    for a in range(2):
        source = pl.ds(a * 128, 128)
        packed = jnp.zeros((32, 128), F32)
        for g in range(32):
            k = g // 8 * 4 + a * 3
            rows = pl.ds(8 + g % 8 * 32, 32)
            to_level = (4 * g + 2 - (126 if a else 0)) % 128
            to_spread = (4 * g + 1 - (127 if a else 0)) % 128
            moved = jnp.where(
                lane % 4 == 1,
                pltpu.roll(spreads[k, rows, source], to_spread, 1),
                pltpu.roll(levels[k, rows, source], to_level, 1),
            )
            if g < 8:
                to_wind = (4 * g - (127 if a else 0)) % 128
                moved = jnp.where(
                    lane % 4 == 0,
                    pltpu.roll(wind[g // 4, pl.ds((g % 4) * 32, 32), :], to_wind, 1),
                    moved,
                )
            packed = jnp.where(lane // 4 == g, moved, packed)
        col_send[a] = packed

    pl.semaphore_wait(barrier, len(OFFSETS) - 1 + 6)

    halos = []
    for b in range(2):
        halos.append(
            pltpu.make_async_remote_copy(
                src_ref=row_send.at[b], dst_ref=row_recv.at[1 - b],
                send_sem=row_sem.at[b], recv_sem=row_rsem.at[1 - b],
                device_id={"gx": gx_at[b], "gy": gy}, device_id_type=MESH,
            )
        )
        halos.append(
            pltpu.make_async_remote_copy(
                src_ref=col_send.at[b], dst_ref=col_recv.at[1 - b],
                send_sem=col_sem.at[b], recv_sem=col_rsem.at[1 - b],
                device_id={"gx": gx, "gy": gy_at[b]}, device_id_type=MESH,
            )
        )
        for a in range(2):
            k = b * 2 + a
            halos.append(
                pltpu.make_async_remote_copy(
                    src_ref=diag_send.at[k], dst_ref=diag_recv.at[3 - k],
                    send_sem=diag_sem.at[k], recv_sem=diag_rsem.at[3 - k],
                    device_id={"gx": gx_at[b], "gy": gy_at[a]}, device_id_type=MESH,
                )
            )
    for copy in halos:
        copy.start()

    def prepare_rest(block, carry):
        for tile_y, halves in ((0, (1,)), (1, (0, 1)), (2, (0, 1)), (3, (0,))):
            prepare(block // 4, tile_y, block % 4, range(8), halves)
        return carry

    for tile_y, halves in ((0, (1,)), (1, (0, 1)), (2, (0, 1)), (3, (0,))):
        prepare(0, tile_y, 0, range(1, 8), halves)
        prepare(3, tile_y, 3, range(7), halves)
    lax.fori_loop(1, 15, prepare_rest, 0)

    edge_lanes = pl.ds(TILE, 128)

    def set_edges(block, carry):
        rows = pl.ds(pl.multiple_of(block % 4 * 64 + 8, 8), 64)
        k = block // 4 * 4
        for ref in (levels, spreads):
            ref[k, rows, edge_lanes] = ref[k + 1, rows, 0:128]
            for t in (1, 2):
                ref[k + t, rows, edge_lanes] = jnp.where(
                    low_lane, ref[k + t + 1, rows, 0:128], ref[k + t - 1, rows, 128:256]
                )
            ref[k + 3, rows, edge_lanes] = ref[k + 2, rows, 128:256]
        return carry

    lax.fori_loop(0, 16, set_edges, 0)

    for c in range(2):
        wind_pad[c, 8 : 8 + COARSE, 0:128] = wind[c]

    column = lax.broadcasted_iota(jnp.int32, (256, RING), 0)
    column = jnp.where(column >= 192, column - 256, column)
    fire = lax.broadcasted_iota(jnp.int32, (256, RING), 1)
    fire = jnp.where(fire >= 320, fire - RING, fire)
    offset = (fire.astype(F32) + 0.5) * (1.0 / REFINE) - 0.5 - column.astype(F32)

    has_row = (gx > 0, gx < N_GX - 1)
    has_col = (gy > 0, gy < N_GY - 1)

    for copy in halos:
        copy.wait()

    cols = [jnp.where(has_col[a], col_recv[a], 0.0) for a in range(2)]
    for g in range(32):
        rows = pl.ds(8 + g % 8 * 32, 32)
        for ref, item, last in ((levels, 2, 126), (spreads, 1, 127)):
            k = g // 8 * 4
            got = pltpu.roll(cols[0], (last - (4 * g + item)) % 128, 1)
            ref[k, rows, edge_lanes] = jnp.where(low_lane, ref[k, rows, edge_lanes], got)
            got = pltpu.roll(cols[1], (0 - (4 * g + item)) % 128, 1)
            ref[k + 3, rows, edge_lanes] = jnp.where(low_lane, got, ref[k + 3, rows, edge_lanes])
        if g < 8:
            ends = [pltpu.roll(cols[a], ((0 if a else 127) - 4 * g) % 128, 1) for a in range(2)]
            wind_pad[g // 4, pl.ds(8 + (g % 4) * 32, 32), 128:256] = jnp.where(
                low_lane, ends[1], ends[0]
            )
    for b in range(2):
        rows = pl.ds(b * (TILE + 8), 8)
        from_rows = pl.ds(8 if b else TILE, 8)
        for k in range(16):
            if k // 4 == b * 3:
                t = k % 4
                for ref, part in ((levels, 0), (spreads, 8)):
                    got = row_recv[b, part : part + 8, :]
                    ref[k, rows, 0:TILE] = jnp.where(has_row[b], got[:, t * TILE : t * TILE + TILE], 0.0)
                    corner = [
                        jnp.where(has_col[a], diag_recv[b * 2 + a, 0:8, :], 0.0) for a in range(2)
                    ]
                    last = corner[0] if t == 0 else got[:, t * TILE - 128 : t * TILE]
                    after = corner[1] if t == 3 else got[:, t * TILE + TILE : t * TILE + TILE + 128]
                    ref[k, rows, edge_lanes] = jnp.where(
                        has_row[b], jnp.where(low_lane, after, last), 0.0
                    )
            else:
                for ref in (levels, spreads):
                    ref[k, rows, :] = ref[k + (4 if b else -4), from_rows, :]
        wind_at = pl.ds(b * (COARSE + 8), 8)
        for c in range(2):
            wind_pad[c, wind_at, 0:128] = jnp.where(
                has_row[b], row_recv[b, c * 8 : c * 8 + 8, SIDE : SIDE + 128], 0.0
            )
            ends = [
                jnp.where(has_col[a], diag_recv[b * 2 + a, 8 + c * 8 : 16 + c * 8, :], 0.0)
                for a in range(2)
            ]
            wind_pad[c, wind_at, 128:256] = jnp.where(
                has_row[b], jnp.where(low_lane, ends[1], ends[0]), 0.0
            )

    for t in range(4):
        weight = jnp.maximum(1.0 - jnp.abs(offset + 32.0 * t), 0.0).astype(BF16)
        for c in range(2):
            high, low = split(dot2(wind_pad[c], weight))
            for tx in range(4):
                lanes = pl.ds(c * RING, RING)
                winds[tx * 4 + t, 0:48, lanes] = high[tx * 32 : tx * 32 + 48]
                winds[tx * 4 + t, 48:96, lanes] = low[tx * 32 : tx * 32 + 48]

    sub = lax.broadcasted_iota(jnp.int32, (8, RING), 0)
    sub_in = lax.broadcasted_iota(jnp.int32, (8, TILE), 0)
    place = jnp.where(
        lax.broadcasted_iota(jnp.int32, (TILE, 128), 0) // REFINE
        == lax.broadcasted_iota(jnp.int32, (TILE, 128), 1),
        1.0,
        0.0,
    ).astype(BF16)

    def eight(i):
        return pl.ds(pl.multiple_of(i * 8, 8), 8)

    def one_part(n, carry):
        c = n // len(OFFSETS)
        j = n % len(OFFSETS)
        ox = jnp.int32(0)
        oy = jnp.int32(0)
        for i, (dx, dy) in enumerate(OFFSETS):
            now = (j == i).astype(jnp.int32)
            ox = ox + now * dx
            oy = oy + now * dy
        target = ((my_x + ox) % 4) * 4 + (my_y + oy) % 4

        chosen = plan[target]
        part = pl.ds(pl.multiple_of(c * PART, PART), PART)
        fire_wind[...] = jnp.dot(
            row_weight[pl.ds(pl.multiple_of(c * PART, PART), PART + 16), :],
            winds[chosen],
            preferred_element_type=F32,
        )

        def level_rows(i):
            return levels[chosen, eight(c * GROUPS + i), :]

        above = centre = level_rows(0)
        for i in range(GROUPS + 2):
            below = level_rows(i + 1) if i < GROUPS + 1 else centre
            up = pltpu.roll(jnp.where(sub == 7, above, centre), 1, 0)
            down = pltpu.roll(jnp.where(sub == 0, below, centre), 7, 0)
            left = pltpu.roll(centre, 1, 1)
            right = pltpu.roll(centre, RING - 1, 1)
            rows = slice(i * 8, i * 8 + 8)
            halfway[rows, :] = advance(
                centre, up, down, left, right,
                fire_wind[rows, 0:RING], fire_wind[rows, RING : 2 * RING],
                spreads[chosen, eight(c * GROUPS + i), :],
            )
            above, centre = centre, below

        above, centre = halfway[0:8, :], halfway[8:16, :]
        for i in range(GROUPS):
            below = halfway[i * 8 + 16 : i * 8 + 24, :]
            inner = centre[:, 0:TILE]
            up = pltpu.roll(jnp.where(sub_in == 7, above[:, 0:TILE], inner), 1, 0)
            down = pltpu.roll(jnp.where(sub_in == 0, below[:, 0:TILE], inner), 7, 0)
            left = pltpu.roll(centre, 1, 1)[:, 0:TILE]
            right = pltpu.roll(centre, RING - 1, 1)[:, 0:TILE]
            rows = slice(i * 8 + 8, i * 8 + 16)
            padded = eight(c * GROUPS + i + 1)
            result = advance(
                inner, up, down, left, right,
                fire_wind[rows, 0:TILE], fire_wind[rows, RING : RING + TILE],
                spreads[chosen, padded, 0:TILE],
            )
            before = jnp.clip(0.5 - levels[chosen, padded, 0:TILE], 0.0, 1.0)
            after = jnp.clip(0.5 - result, 0.0, 1.0)
            heat = lookup(
                heat_table, 1.0 / (2.0 * TIME_STEP * REFINE * REFINE), fuels[chosen, eight(c * GROUPS + i), :]
            )
            released = heat * (after - before)
            release[0, i * 8 : i * 8 + 8, :] = released[:, 0:128]
            release[1, i * 8 : i * 8 + 8, :] = released[:, 128:256]
            stage[target, eight(c * GROUPS + i), :] = result
            above, centre = centre, below

        @pl.when(j < len(OFFSETS) - 1)
        def _():
            pltpu.make_async_remote_copy(
                src_ref=stage.at[target, part], dst_ref=out.at[gx, part],
                send_sem=send_sem.at[j, c], recv_sem=recv_sem.at[j, c],
                device_id={"gx": target, "gy": gy}, device_id_type=MESH,
            ).start()

        sums = []
        for half in range(2):
            total = release[half, pl.ds(0, GROUPS, stride=8), :]
            for s in range(1, 8):
                total = total + release[half, pl.ds(s, GROUPS, stride=8), :]
            sums.append(total)
        flux[target, pl.ds(pl.multiple_of(c * GROUPS, GROUPS), GROUPS), :] = dot2(
            jnp.concatenate(sums, axis=1), place
        )
        return carry

    lax.fori_loop(0, PARTS * len(OFFSETS), one_part, 0)

    own = pltpu.make_async_copy(stage.at[gx], out.at[gx], own_sem)
    own.start()

    for tx in range(4):
        band = jnp.zeros((32, 128), F32)
        for ty in range(4):
            band = band + pltpu.roll(flux[plan[16 + tx * 4 + ty]], ty * 32, 1)
        for l in range(LEV):
            heating[l, tx * 32 : tx * 32 + 32, :] = profile[l] * band

    own.wait()

    def finish(j, carry):
        for c in range(PARTS):
            part = pl.ds(c * PART, PART)
            pltpu.make_async_remote_copy(
                src_ref=stage.at[gx, part], dst_ref=out.at[gx, part],
                send_sem=send_sem.at[j, c], recv_sem=recv_sem.at[j, c],
                device_id={"gx": (gx + 1) % N_GX, "gy": gy}, device_id_type=MESH,
            ).wait()
        return carry

    lax.fori_loop(0, len(OFFSETS) - 1, finish, 0)


def body(
    level_set, fuel_class, ignition, counts, destination, surface_wind, spread_table, heat_table, profile
):
    hbm = pl.BlockSpec(memory_space=pltpu.HBM)
    vmem = pl.BlockSpec(memory_space=pltpu.VMEM)
    dma = pltpu.SemaphoreType.DMA

    target = jnp.where(counts > 0, destination, 16).reshape(16)
    ids = jnp.arange(16, dtype=jnp.int32)
    taken = jnp.min(jnp.where(target[None, :] == ids[:, None], ids[None, :], 16), axis=1)
    plan = jnp.concatenate([taken, target])

    relocated, heating = pl.pallas_call(
        kernel,
        out_shape=(
            jax.ShapeDtypeStruct((N_GX, TILE, TILE), F32),
            jax.ShapeDtypeStruct((LEV, COARSE, COARSE), F32),
        ),
        in_specs=[hbm] * 8,
        out_specs=(vmem, vmem),
        scratch_shapes=[
            pltpu.VMEM((17, TILE + 16, RING), F32),
            pltpu.VMEM((17, TILE + 16, RING), F32),
            pltpu.VMEM((17, TILE, TILE), jnp.int32),
            pltpu.VMEM((17, 96, 2 * RING), BF16),
            pltpu.VMEM((PART + 16, RING), F32),
            pltpu.VMEM((PART + 16, 2 * RING), F32),
            pltpu.VMEM((COARSE, COARSE), jnp.int32),
            pltpu.VMEM((2, COARSE, COARSE), F32),
            pltpu.SMEM((NFUEL,), F32),
            pltpu.SMEM((NFUEL,), F32),
            pltpu.SMEM((32,), jnp.int32),
            pltpu.SMEM((LEV,), F32),
            pltpu.VMEM((2, COARSE + 16, 256), F32),
            pltpu.VMEM((TILE + 16, 96), BF16),
            pltpu.VMEM((4, COARSE, TILE), F32),
            pltpu.VMEM((N_GX, TILE, TILE), F32),
            pltpu.VMEM((2, PART, 128), F32),
            pltpu.VMEM((17, 32, 128), F32),
            pltpu.VMEM((2, 16, SIDE + 128), F32),
            pltpu.VMEM((2, 16, SIDE + 128), F32),
            pltpu.VMEM((2, 32, 128), F32),
            pltpu.VMEM((2, 32, 128), F32),
            pltpu.VMEM((4, 24, 128), F32),
            pltpu.VMEM((4, 24, 128), F32),
            dma((6,)),
            dma((16,)),
            dma((16,)),
            dma((2,)),
            dma((2,)),
            dma((4,)),
            dma((2,)),
            dma((2,)),
            dma((4,)),
            dma((16, PARTS)),
            dma((16, PARTS)),
            dma,
        ],
        compiler_params=pltpu.CompilerParams(
            collective_id=0, has_side_effects=True, vmem_limit_bytes=49 << 20
        ),
    )(
        level_set, fuel_class, ignition, surface_wind, spread_table, heat_table, plan, profile
    )
    return relocated.reshape(1, N_GX, TILE, TILE), heating


def solution(mesh):
    in_specs = (
        P("gx", "gy"),
        P("gx", "gy"),
        P("gx", "gy"),
        P("gx", "gy"),
        P("gx", "gy"),
        P(None, "gx", "gy"),
        P(),
        P(),
        P(),
    )
    out_specs = (P("gy", "gx", None, None), P(None, "gx", "gy"))
    return jax.shard_map(body, mesh=mesh, in_specs=in_specs, out_specs=out_specs, check_vma=False)
```

```python
import jax
import jax.numpy as jnp
from jax import lax
from jax.experimental import pallas as pl
from jax.experimental.pallas import tpu as pltpu
from jax.sharding import PartitionSpec as P

TILE = 256
REFINE = 8
NFUEL = 13
LEV = 4
TIME_STEP = 0.6
IGNITE_DEPTH = 1.5
N_GX = 16
N_GY = 8
SIDE = 1024
COARSE = 128
RING = 384
TINY = 1e-30
PARTS = 4
PART = TILE // PARTS
GROUPS = PART // 8
MESH = pl.DeviceIdType.MESH
F32 = jnp.float32
BF16 = jnp.bfloat16

OFFSETS = ((2, 2), (0, 1), (1, 0), (0, 3), (3, 0), (2, 1), (1, 2), (2, 3), (3, 2), (0, 2), (2, 0), (1, 1), (3, 3), (1, 3), (3, 1), (0, 0))


def split(x):
    high = x.astype(BF16)
    return high, (x - high.astype(F32)).astype(BF16)


def dot2(a, b):
    high, low = split(a)
    return jnp.dot(high, b, preferred_element_type=F32) + jnp.dot(
        low, b, preferred_element_type=F32
    )


def advance(centre, up, down, left, right, wind_x, wind_y, reach):
    back_x = centre - up
    ahead_x = down - centre
    back_y = centre - left
    ahead_y = right - centre
    twice_x = down - up
    twice_y = right - left
    push = jnp.maximum(wind_x * twice_x + wind_y * twice_y, 0.0)
    push2 = push * push
    whole = twice_x * twice_x + twice_y * twice_y + 4.0 + push2
    gain = whole + 2.0 * push2
    px = jnp.maximum(back_x, 0.0)
    nx = jnp.minimum(ahead_x, 0.0)
    py = jnp.maximum(back_y, 0.0)
    ny = jnp.minimum(ahead_y, 0.0)
    upwind2 = (px * px + nx * nx) + (py * py + ny * ny)
    scale = lax.rsqrt(jnp.maximum(upwind2, TINY) * (whole * whole))
    return centre - (reach * gain) * (upwind2 * scale)


def lookup(table, scale, codes):
    values = [table[t] * scale for t in range(NFUEL)]
    bit = 1
    while len(values) > 1:
        odd = (codes & bit) != 0
        values = [
            jnp.where(odd, values[t + 1], values[t]) if t + 1 < len(values) else values[t]
            for t in range(0, len(values), 2)
        ]
        bit *= 2
    return values[0]


def kernel(
    level_hbm, fuel_hbm, ignition_hbm, wind_hbm, spread_hbm, heat_hbm, plan_hbm, profile_hbm,
    out, heating,
    levels, spreads, fuels, winds, halfway, fire_wind,
    ignition, wind, spread_table, heat_table, plan, profile,
    wind_pad, row_weight, ignite, stage, release, flux,
    row_send, row_recv, col_send, col_recv, diag_send, diag_recv,
    small_sem, level_sem, fuel_sem,
    row_sem, col_sem, diag_sem, row_rsem, col_rsem, diag_rsem, send_sem, recv_sem, own_sem,
):
    gx = lax.axis_index("gx")
    gy = lax.axis_index("gy")
    my_x = gx // 4
    my_y = gx % 4
    gx_at = ((gx + N_GX - 1) % N_GX, (gx + 1) % N_GX)
    gy_at = ((gy + N_GY - 1) % N_GY, (gy + 1) % N_GY)

    small = [
        pltpu.make_async_copy(source, here, small_sem.at[n])
        for n, (source, here) in enumerate((
            (ignition_hbm, ignition), (spread_hbm, spread_table), (wind_hbm, wind),
            (heat_hbm, heat_table), (plan_hbm, plan), (profile_hbm, profile),
        ))
    ]
    for copy in small:
        copy.start()
    loads = []
    for k in range(16):
        block = (pl.ds(k // 4 * TILE, TILE), pl.ds(k % 4 * TILE, TILE))
        loads.append(
            pltpu.make_async_copy(
                level_hbm.at[block], levels.at[k, pl.ds(8, TILE), pl.ds(0, TILE)], level_sem.at[k]
            )
        )
        loads.append(pltpu.make_async_copy(fuel_hbm.at[block], fuels.at[k], fuel_sem.at[k]))
    for copy in loads:
        copy.start()

    barrier = pltpu.get_barrier_semaphore()
    for ox, oy in OFFSETS[:-1]:
        peer = ((my_x + ox) % 4) * 4 + (my_y + oy) % 4
        pl.semaphore_signal(
            barrier, inc=1, device_id={"gx": peer, "gy": gy}, device_id_type=MESH
        )
    for b in range(2):
        for px in (gx, gx_at[0], gx_at[1]):
            pl.semaphore_signal(
                barrier, inc=1, device_id={"gx": px, "gy": gy_at[b]}, device_id_type=MESH
            )

    lane = lax.broadcasted_iota(jnp.int32, (1, 128), 1)
    low_lane = lane < 64

    levels[16] = jnp.zeros((TILE + 16, RING), F32)
    spreads[16] = jnp.zeros((TILE + 16, RING), F32)
    fuels[16] = jnp.zeros((TILE, TILE), jnp.int32)
    winds[16] = jnp.zeros((96, 2 * RING), BF16)
    flux[16] = jnp.zeros((32, 128), F32)

    fire_row = (lax.broadcasted_iota(jnp.int32, (TILE + 16, 96), 0) - 8).astype(F32)
    coarse_row = lax.broadcasted_iota(jnp.int32, (TILE + 16, 96), 1)
    coarse_row = (jnp.where(coarse_row >= 48, coarse_row - 48, coarse_row) - 8).astype(F32)
    tent = 1.0 - jnp.abs((fire_row + 0.5) * (1.0 / REFINE) - 0.5 - coarse_row)
    row_weight[...] = jnp.maximum(tent, 0.0).astype(BF16)

    for copy in small:
        copy.wait()
    cell = lax.broadcasted_iota(jnp.int32, (COARSE, TILE), 0)
    at = lax.broadcasted_iota(jnp.int32, (COARSE, TILE), 1) // REFINE
    burning = ignition[...].astype(F32).astype(BF16)
    for t in range(4):
        repeat = jnp.where(cell == at + t * 32, IGNITE_DEPTH, 0.0).astype(BF16)
        ignite[t] = jnp.dot(burning, repeat, preferred_element_type=F32)

    def prepare(tile_x, tile_y, block, subs, halves):
        k = tile_x * 4 + tile_y
        for half in halves:
            lanes = pl.ds(half * 128, 128)
            burned = ignite[tile_y, pl.ds(pl.multiple_of(tile_x * 32 + block * 8, 8), 8), lanes]
            for s in subs:
                inner = pl.ds(pl.multiple_of(block * 64 + s * 8 + 8, 8), 8)
                levels[k, inner, lanes] = levels[k, inner, lanes] - burned[s : s + 1, :]
                codes = fuels[k, pl.ds(pl.multiple_of(block * 64 + s * 8, 8), 8), lanes]
                spreads[k, inner, lanes] = lookup(spread_table, TIME_STEP, codes)

    for copy in loads:
        copy.wait()

    def prepare_edges(block, carry):
        prepare(block // 4, 0, block % 4, range(8), (0,))
        prepare(block // 4, 3, block % 4, range(8), (1,))
        return carry

    lax.fori_loop(0, 16, prepare_edges, 0)
    for tile_y, halves in ((0, (1,)), (1, (0, 1)), (2, (0, 1)), (3, (0,))):
        prepare(0, tile_y, 0, (0,), halves)
        prepare(3, tile_y, 3, (7,), halves)

    wind_edges = (0, COARSE - 8)
    for b in range(2):
        rows = pl.ds(b * (TILE - 8) + 8, 8)
        for t in range(4):
            lanes = pl.ds(t * TILE, TILE)
            row_send[b, 0:8, lanes] = levels[b * 12 + t, rows, 0:TILE]
            row_send[b, 8:16, lanes] = spreads[b * 12 + t, rows, 0:TILE]
        for c in range(2):
            row_send[b, c * 8 : c * 8 + 8, SIDE : SIDE + 128] = wind[c, pl.ds(wind_edges[b], 8), :]
        for a in range(2):
            diag_send[b * 2 + a, 0:8, :] = levels[b * 12 + a * 3, rows, pl.ds(a * 128, 128)]
            for c in range(2):
                diag_send[b * 2 + a, 8 + c * 8 : 16 + c * 8, :] = wind[c, pl.ds(wind_edges[b], 8), :]
    for a in range(2):
        source = pl.ds(a * 128, 128)
        packed = jnp.zeros((32, 128), F32)
        for g in range(32):
            k = g // 8 * 4 + a * 3
            rows = pl.ds(8 + g % 8 * 32, 32)
            to_level = (4 * g + 2 - (126 if a else 0)) % 128
            to_spread = (4 * g + 1 - (127 if a else 0)) % 128
            moved = jnp.where(
                lane % 4 == 1,
                pltpu.roll(spreads[k, rows, source], to_spread, 1),
                pltpu.roll(levels[k, rows, source], to_level, 1),
            )
            if g < 8:
                to_wind = (4 * g - (127 if a else 0)) % 128
                moved = jnp.where(
                    lane % 4 == 0,
                    pltpu.roll(wind[g // 4, pl.ds((g % 4) * 32, 32), :], to_wind, 1),
                    moved,
                )
            packed = jnp.where(lane // 4 == g, moved, packed)
        col_send[a] = packed

    pl.semaphore_wait(barrier, len(OFFSETS) - 1 + 6)

    halos = []
    for b in range(2):
        halos.append(
            pltpu.make_async_remote_copy(
                src_ref=row_send.at[b], dst_ref=row_recv.at[1 - b],
                send_sem=row_sem.at[b], recv_sem=row_rsem.at[1 - b],
                device_id={"gx": gx_at[b], "gy": gy}, device_id_type=MESH,
            )
        )
        halos.append(
            pltpu.make_async_remote_copy(
                src_ref=col_send.at[b], dst_ref=col_recv.at[1 - b],
                send_sem=col_sem.at[b], recv_sem=col_rsem.at[1 - b],
                device_id={"gx": gx, "gy": gy_at[b]}, device_id_type=MESH,
            )
        )
        for a in range(2):
            k = b * 2 + a
            halos.append(
                pltpu.make_async_remote_copy(
                    src_ref=diag_send.at[k], dst_ref=diag_recv.at[3 - k],
                    send_sem=diag_sem.at[k], recv_sem=diag_rsem.at[3 - k],
                    device_id={"gx": gx_at[b], "gy": gy_at[a]}, device_id_type=MESH,
                )
            )
    for copy in halos:
        copy.start()

    def prepare_rest(block, carry):
        for tile_y, halves in ((0, (1,)), (1, (0, 1)), (2, (0, 1)), (3, (0,))):
            prepare(block // 4, tile_y, block % 4, range(8), halves)
        return carry

    for tile_y, halves in ((0, (1,)), (1, (0, 1)), (2, (0, 1)), (3, (0,))):
        prepare(0, tile_y, 0, range(1, 8), halves)
        prepare(3, tile_y, 3, range(7), halves)
    lax.fori_loop(1, 15, prepare_rest, 0)

    edge_lanes = pl.ds(TILE, 128)

    def set_edges(block, carry):
        rows = pl.ds(pl.multiple_of(block % 4 * 64 + 8, 8), 64)
        k = block // 4 * 4
        for ref in (levels, spreads):
            ref[k, rows, edge_lanes] = ref[k + 1, rows, 0:128]
            for t in (1, 2):
                ref[k + t, rows, edge_lanes] = jnp.where(
                    low_lane, ref[k + t + 1, rows, 0:128], ref[k + t - 1, rows, 128:256]
                )
            ref[k + 3, rows, edge_lanes] = ref[k + 2, rows, 128:256]
        return carry

    lax.fori_loop(0, 16, set_edges, 0)

    for c in range(2):
        wind_pad[c, 8 : 8 + COARSE, 0:128] = wind[c]

    column = lax.broadcasted_iota(jnp.int32, (256, RING), 0)
    column = jnp.where(column >= 192, column - 256, column)
    fire = lax.broadcasted_iota(jnp.int32, (256, RING), 1)
    fire = jnp.where(fire >= 320, fire - RING, fire)
    offset = (fire.astype(F32) + 0.5) * (1.0 / REFINE) - 0.5 - column.astype(F32)

    has_row = (gx > 0, gx < N_GX - 1)
    has_col = (gy > 0, gy < N_GY - 1)

    for copy in halos:
        copy.wait()

    cols = [jnp.where(has_col[a], col_recv[a], 0.0) for a in range(2)]
    for g in range(32):
        rows = pl.ds(8 + g % 8 * 32, 32)
        for ref, item, last in ((levels, 2, 126), (spreads, 1, 127)):
            k = g // 8 * 4
            got = pltpu.roll(cols[0], (last - (4 * g + item)) % 128, 1)
            ref[k, rows, edge_lanes] = jnp.where(low_lane, ref[k, rows, edge_lanes], got)
            got = pltpu.roll(cols[1], (0 - (4 * g + item)) % 128, 1)
            ref[k + 3, rows, edge_lanes] = jnp.where(low_lane, got, ref[k + 3, rows, edge_lanes])
        if g < 8:
            ends = [pltpu.roll(cols[a], ((0 if a else 127) - 4 * g) % 128, 1) for a in range(2)]
            wind_pad[g // 4, pl.ds(8 + (g % 4) * 32, 32), 128:256] = jnp.where(
                low_lane, ends[1], ends[0]
            )
    for b in range(2):
        rows = pl.ds(b * (TILE + 8), 8)
        from_rows = pl.ds(8 if b else TILE, 8)
        for k in range(16):
            if k // 4 == b * 3:
                t = k % 4
                for ref, part in ((levels, 0), (spreads, 8)):
                    got = row_recv[b, part : part + 8, :]
                    ref[k, rows, 0:TILE] = jnp.where(has_row[b], got[:, t * TILE : t * TILE + TILE], 0.0)
                    corner = [
                        jnp.where(has_col[a], diag_recv[b * 2 + a, 0:8, :], 0.0) for a in range(2)
                    ]
                    last = corner[0] if t == 0 else got[:, t * TILE - 128 : t * TILE]
                    after = corner[1] if t == 3 else got[:, t * TILE + TILE : t * TILE + TILE + 128]
                    ref[k, rows, edge_lanes] = jnp.where(
                        has_row[b], jnp.where(low_lane, after, last), 0.0
                    )
            else:
                for ref in (levels, spreads):
                    ref[k, rows, :] = ref[k + (4 if b else -4), from_rows, :]
        wind_at = pl.ds(b * (COARSE + 8), 8)
        for c in range(2):
            wind_pad[c, wind_at, 0:128] = jnp.where(
                has_row[b], row_recv[b, c * 8 : c * 8 + 8, SIDE : SIDE + 128], 0.0
            )
            ends = [
                jnp.where(has_col[a], diag_recv[b * 2 + a, 8 + c * 8 : 16 + c * 8, :], 0.0)
                for a in range(2)
            ]
            wind_pad[c, wind_at, 128:256] = jnp.where(
                has_row[b], jnp.where(low_lane, ends[1], ends[0]), 0.0
            )

    for t in range(4):
        weight = jnp.maximum(1.0 - jnp.abs(offset + 32.0 * t), 0.0).astype(BF16)
        for c in range(2):
            high, low = split(dot2(wind_pad[c], weight))
            for tx in range(4):
                lanes = pl.ds(c * RING, RING)
                winds[tx * 4 + t, 0:48, lanes] = high[tx * 32 : tx * 32 + 48]
                winds[tx * 4 + t, 48:96, lanes] = low[tx * 32 : tx * 32 + 48]

    sub = lax.broadcasted_iota(jnp.int32, (8, RING), 0)
    sub_in = lax.broadcasted_iota(jnp.int32, (8, TILE), 0)
    place = jnp.where(
        lax.broadcasted_iota(jnp.int32, (TILE, 128), 0) // REFINE
        == lax.broadcasted_iota(jnp.int32, (TILE, 128), 1),
        1.0,
        0.0,
    ).astype(BF16)

    def eight(i):
        return pl.ds(pl.multiple_of(i * 8, 8), 8)

    def one_part(n, carry):
        c = n // len(OFFSETS)
        j = n % len(OFFSETS)
        ox = jnp.int32(0)
        oy = jnp.int32(0)
        for i, (dx, dy) in enumerate(OFFSETS):
            now = (j == i).astype(jnp.int32)
            ox = ox + now * dx
            oy = oy + now * dy
        target = ((my_x + ox) % 4) * 4 + (my_y + oy) % 4

        chosen = plan[target]
        part = pl.ds(pl.multiple_of(c * PART, PART), PART)
        fire_wind[...] = jnp.dot(
            row_weight[pl.ds(pl.multiple_of(c * PART, PART), PART + 16), :],
            winds[chosen],
            preferred_element_type=F32,
        )

        def level_rows(i):
            return levels[chosen, eight(c * GROUPS + i), :]

        above = centre = level_rows(0)
        for i in range(GROUPS + 2):
            below = level_rows(i + 1) if i < GROUPS + 1 else centre
            up = pltpu.roll(jnp.where(sub == 7, above, centre), 1, 0)
            down = pltpu.roll(jnp.where(sub == 0, below, centre), 7, 0)
            left = pltpu.roll(centre, 1, 1)
            right = pltpu.roll(centre, RING - 1, 1)
            rows = slice(i * 8, i * 8 + 8)
            halfway[rows, :] = advance(
                centre, up, down, left, right,
                fire_wind[rows, 0:RING], fire_wind[rows, RING : 2 * RING],
                spreads[chosen, eight(c * GROUPS + i), :],
            )
            above, centre = centre, below

        above, centre = halfway[0:8, :], halfway[8:16, :]
        for i in range(GROUPS):
            below = halfway[i * 8 + 16 : i * 8 + 24, :]
            inner = centre[:, 0:TILE]
            up = pltpu.roll(jnp.where(sub_in == 7, above[:, 0:TILE], inner), 1, 0)
            down = pltpu.roll(jnp.where(sub_in == 0, below[:, 0:TILE], inner), 7, 0)
            left = pltpu.roll(centre, 1, 1)[:, 0:TILE]
            right = pltpu.roll(centre, RING - 1, 1)[:, 0:TILE]
            rows = slice(i * 8 + 8, i * 8 + 16)
            padded = eight(c * GROUPS + i + 1)
            result = advance(
                inner, up, down, left, right,
                fire_wind[rows, 0:TILE], fire_wind[rows, RING : RING + TILE],
                spreads[chosen, padded, 0:TILE],
            )
            before = jnp.clip(0.5 - levels[chosen, padded, 0:TILE], 0.0, 1.0)
            after = jnp.clip(0.5 - result, 0.0, 1.0)
            heat = lookup(
                heat_table, 1.0 / (2.0 * TIME_STEP * REFINE * REFINE), fuels[chosen, eight(c * GROUPS + i), :]
            )
            released = heat * (after - before)
            release[0, i * 8 : i * 8 + 8, :] = released[:, 0:128]
            release[1, i * 8 : i * 8 + 8, :] = released[:, 128:256]
            stage[target, eight(c * GROUPS + i), :] = result
            above, centre = centre, below

        @pl.when(j < len(OFFSETS) - 1)
        def _():
            pltpu.make_async_remote_copy(
                src_ref=stage.at[target, part], dst_ref=out.at[gx, part],
                send_sem=send_sem.at[j, c], recv_sem=recv_sem.at[j, c],
                device_id={"gx": target, "gy": gy}, device_id_type=MESH,
            ).start()

        sums = []
        for half in range(2):
            total = release[half, pl.ds(0, GROUPS, stride=8), :]
            for s in range(1, 8):
                total = total + release[half, pl.ds(s, GROUPS, stride=8), :]
            sums.append(total)
        flux[target, pl.ds(pl.multiple_of(c * GROUPS, GROUPS), GROUPS), :] = dot2(
            jnp.concatenate(sums, axis=1), place
        )
        return carry

    lax.fori_loop(0, PARTS * len(OFFSETS), one_part, 0)

    own = pltpu.make_async_copy(stage.at[gx], out.at[gx], own_sem)
    own.start()

    for tx in range(4):
        band = jnp.zeros((32, 128), F32)
        for ty in range(4):
            band = band + pltpu.roll(flux[plan[16 + tx * 4 + ty]], ty * 32, 1)
        for l in range(LEV):
            heating[l, tx * 32 : tx * 32 + 32, :] = profile[l] * band

    own.wait()

    def finish(j, carry):
        for c in range(PARTS):
            part = pl.ds(c * PART, PART)
            pltpu.make_async_remote_copy(
                src_ref=stage.at[gx, part], dst_ref=out.at[gx, part],
                send_sem=send_sem.at[j, c], recv_sem=recv_sem.at[j, c],
                device_id={"gx": (gx + 1) % N_GX, "gy": gy}, device_id_type=MESH,
            ).wait()
        return carry

    lax.fori_loop(0, len(OFFSETS) - 1, finish, 0)


def body(
    level_set, fuel_class, ignition, counts, destination, surface_wind, spread_table, heat_table, profile
):
    hbm = pl.BlockSpec(memory_space=pltpu.HBM)
    vmem = pl.BlockSpec(memory_space=pltpu.VMEM)
    dma = pltpu.SemaphoreType.DMA

    target = jnp.where(counts > 0, destination, 16).reshape(16)
    ids = jnp.arange(16, dtype=jnp.int32)
    taken = jnp.min(jnp.where(target[None, :] == ids[:, None], ids[None, :], 16), axis=1)
    plan = jnp.concatenate([taken, target])

    ignition, surface_wind, spread_table, heat_table, profile = (
        pltpu.with_memory_space_constraint(x, pltpu.HBM)
        for x in (ignition, surface_wind, spread_table, heat_table, profile)
    )
    relocated, heating = pl.pallas_call(
        kernel,
        out_shape=(
            jax.ShapeDtypeStruct((N_GX, TILE, TILE), F32),
            jax.ShapeDtypeStruct((LEV, COARSE, COARSE), F32),
        ),
        in_specs=[hbm] * 8,
        out_specs=(vmem, vmem),
        scratch_shapes=[
            pltpu.VMEM((17, TILE + 16, RING), F32),
            pltpu.VMEM((17, TILE + 16, RING), F32),
            pltpu.VMEM((17, TILE, TILE), jnp.int32),
            pltpu.VMEM((17, 96, 2 * RING), BF16),
            pltpu.VMEM((PART + 16, RING), F32),
            pltpu.VMEM((PART + 16, 2 * RING), F32),
            pltpu.VMEM((COARSE, COARSE), jnp.int32),
            pltpu.VMEM((2, COARSE, COARSE), F32),
            pltpu.SMEM((NFUEL,), F32),
            pltpu.SMEM((NFUEL,), F32),
            pltpu.SMEM((32,), jnp.int32),
            pltpu.SMEM((LEV,), F32),
            pltpu.VMEM((2, COARSE + 16, 256), F32),
            pltpu.VMEM((TILE + 16, 96), BF16),
            pltpu.VMEM((4, COARSE, TILE), F32),
            pltpu.VMEM((N_GX, TILE, TILE), F32),
            pltpu.VMEM((2, PART, 128), F32),
            pltpu.VMEM((17, 32, 128), F32),
            pltpu.VMEM((2, 16, SIDE + 128), F32),
            pltpu.VMEM((2, 16, SIDE + 128), F32),
            pltpu.VMEM((2, 32, 128), F32),
            pltpu.VMEM((2, 32, 128), F32),
            pltpu.VMEM((4, 24, 128), F32),
            pltpu.VMEM((4, 24, 128), F32),
            dma((6,)),
            dma((16,)),
            dma((16,)),
            dma((2,)),
            dma((2,)),
            dma((4,)),
            dma((2,)),
            dma((2,)),
            dma((4,)),
            dma((16, PARTS)),
            dma((16, PARTS)),
            dma,
        ],
        compiler_params=pltpu.CompilerParams(
            collective_id=0, has_side_effects=True, vmem_limit_bytes=49 << 20
        ),
    )(
        level_set, fuel_class, ignition, surface_wind, spread_table, heat_table, plan, profile
    )
    return relocated.reshape(1, N_GX, TILE, TILE), heating


def solution(mesh):
    in_specs = (
        P("gx", "gy"),
        P("gx", "gy"),
        P("gx", "gy"),
        P("gx", "gy"),
        P("gx", "gy"),
        P(None, "gx", "gy"),
        P(),
        P(),
        P(),
    )
    out_specs = (P("gy", "gx", None, None), P(None, "gx", "gy"))
    return jax.shard_map(body, mesh=mesh, in_specs=in_specs, out_specs=out_specs, check_vma=False)
```

```python
import jax
import jax.numpy as jnp
from jax import lax
from jax.experimental import pallas as pl
from jax.experimental.pallas import tpu as pltpu
from jax.sharding import PartitionSpec as P

TILE = 256
REFINE = 8
NFUEL = 13
LEV = 4
TIME_STEP = 0.6
IGNITE_DEPTH = 1.5
N_GX = 16
N_GY = 8
SIDE = 1024
COARSE = 128
RING = 384
TINY = 1e-30
PARTS = 4
PART = TILE // PARTS
GROUPS = PART // 8
EDGE_FIRST = (0, 3, 4, 7, 8, 11, 12, 15, 1, 2, 13, 14, 5, 6, 9, 10)
MESH = pl.DeviceIdType.MESH
F32 = jnp.float32
BF16 = jnp.bfloat16

OFFSETS = ((2, 2), (0, 1), (1, 0), (0, 3), (3, 0), (2, 1), (1, 2), (2, 3), (3, 2), (0, 2), (2, 0), (1, 1), (3, 3), (1, 3), (3, 1), (0, 0))


def split(x):
    high = x.astype(BF16)
    return high, (x - high.astype(F32)).astype(BF16)


def dot2(a, b):
    high, low = split(a)
    return jnp.dot(high, b, preferred_element_type=F32) + jnp.dot(
        low, b, preferred_element_type=F32
    )


def advance(centre, up, down, left, right, wind_x, wind_y, reach):
    back_x = centre - up
    ahead_x = down - centre
    back_y = centre - left
    ahead_y = right - centre
    twice_x = down - up
    twice_y = right - left
    push = jnp.maximum(wind_x * twice_x + wind_y * twice_y, 0.0)
    push2 = push * push
    whole = twice_x * twice_x + twice_y * twice_y + 4.0 + push2
    gain = whole + 2.0 * push2
    px = jnp.maximum(back_x, 0.0)
    nx = jnp.minimum(ahead_x, 0.0)
    py = jnp.maximum(back_y, 0.0)
    ny = jnp.minimum(ahead_y, 0.0)
    upwind2 = (px * px + nx * nx) + (py * py + ny * ny)
    scale = lax.rsqrt(jnp.maximum(upwind2, TINY) * (whole * whole))
    return centre - (reach * gain) * (upwind2 * scale)


def lookup(table, scale, codes):
    values = [table[t] * scale for t in range(NFUEL)]
    bit = 1
    while len(values) > 1:
        odd = (codes & bit) != 0
        values = [
            jnp.where(odd, values[t + 1], values[t]) if t + 1 < len(values) else values[t]
            for t in range(0, len(values), 2)
        ]
        bit *= 2
    return values[0]


def kernel(
    level_hbm, fuel_hbm, ignition_hbm, wind_hbm, spread_hbm, heat_hbm, destination_hbm, profile_hbm,
    out, heating,
    levels, spreads, fuels, winds, halfway, fire_wind,
    ignition, wind, spread_table, heat_table, destination, profile, plan,
    wind_pad, row_weight, ignite, stage, release, flux,
    row_send, row_recv, col_send, col_recv, diag_send, diag_recv,
    small_sem, level_sem, fuel_sem,
    row_sem, col_sem, diag_sem, row_rsem, col_rsem, diag_rsem, send_sem, recv_sem, own_sem,
):
    gx = lax.axis_index("gx")
    gy = lax.axis_index("gy")
    my_x = gx // 4
    my_y = gx % 4
    gx_at = ((gx + N_GX - 1) % N_GX, (gx + 1) % N_GX)
    gy_at = ((gy + N_GY - 1) % N_GY, (gy + 1) % N_GY)

    small = [
        pltpu.make_async_copy(source, here, small_sem.at[n])
        for n, (source, here) in enumerate((
            (ignition_hbm, ignition), (spread_hbm, spread_table), (wind_hbm, wind),
            (heat_hbm, heat_table), (destination_hbm, destination), (profile_hbm, profile),
        ))
    ]
    for copy in small:
        copy.start()
    loads = []
    for k in EDGE_FIRST:
        block = (pl.ds(k // 4 * TILE, TILE), pl.ds(k % 4 * TILE, TILE))
        loads.append(
            pltpu.make_async_copy(
                level_hbm.at[block], levels.at[k, pl.ds(8, TILE), pl.ds(0, TILE)], level_sem.at[k]
            )
        )
        loads.append(pltpu.make_async_copy(fuel_hbm.at[block], fuels.at[k], fuel_sem.at[k]))
    for copy in loads:
        copy.start()

    barrier = pltpu.get_barrier_semaphore()
    for ox, oy in OFFSETS[:-1]:
        peer = ((my_x + ox) % 4) * 4 + (my_y + oy) % 4
        pl.semaphore_signal(
            barrier, inc=1, device_id={"gx": peer, "gy": gy}, device_id_type=MESH
        )
    for b in range(2):
        for px in (gx, gx_at[0], gx_at[1]):
            pl.semaphore_signal(
                barrier, inc=1, device_id={"gx": px, "gy": gy_at[b]}, device_id_type=MESH
            )

    lane = lax.broadcasted_iota(jnp.int32, (1, 128), 1)
    low_lane = lane < 64

    levels[16] = jnp.zeros((TILE + 16, RING), F32)
    spreads[16] = jnp.zeros((TILE + 16, RING), F32)
    fuels[16] = jnp.zeros((TILE, TILE), jnp.int32)
    winds[16] = jnp.zeros((96, 2 * RING), BF16)
    flux[16] = jnp.zeros((32, 128), F32)

    fire_row = (lax.broadcasted_iota(jnp.int32, (TILE + 16, 96), 0) - 8).astype(F32)
    coarse_row = lax.broadcasted_iota(jnp.int32, (TILE + 16, 96), 1)
    coarse_row = (jnp.where(coarse_row >= 48, coarse_row - 48, coarse_row) - 8).astype(F32)
    tent = 1.0 - jnp.abs((fire_row + 0.5) * (1.0 / REFINE) - 0.5 - coarse_row)
    row_weight[...] = jnp.maximum(tent, 0.0).astype(BF16)

    for copy in small:
        copy.wait()
    goes = [destination[k // 4, k % 4] for k in range(16)]
    for k in range(16):
        plan[16 + k] = goes[k] + 17 * (goes[k] < 0).astype(jnp.int32)
    for d in range(16):
        taken = jnp.int32(16)
        for k in range(16):
            taken = taken + (goes[k] == d).astype(jnp.int32) * (k - taken)
        plan[d] = taken
    cell = lax.broadcasted_iota(jnp.int32, (COARSE, TILE), 0)
    at = lax.broadcasted_iota(jnp.int32, (COARSE, TILE), 1) // REFINE
    burning = ignition[...].astype(F32).astype(BF16)
    for t in range(4):
        repeat = jnp.where(cell == at + t * 32, IGNITE_DEPTH, 0.0).astype(BF16)
        ignite[t] = jnp.dot(burning, repeat, preferred_element_type=F32)

    def prepare(tile_x, tile_y, block, subs, halves):
        k = tile_x * 4 + tile_y
        for half in halves:
            lanes = pl.ds(half * 128, 128)
            burned = ignite[tile_y, pl.ds(pl.multiple_of(tile_x * 32 + block * 8, 8), 8), lanes]
            for s in subs:
                inner = pl.ds(pl.multiple_of(block * 64 + s * 8 + 8, 8), 8)
                levels[k, inner, lanes] = levels[k, inner, lanes] - burned[s : s + 1, :]
                codes = fuels[k, pl.ds(pl.multiple_of(block * 64 + s * 8, 8), 8), lanes]
                spreads[k, inner, lanes] = lookup(spread_table, TIME_STEP, codes)

    for copy in loads[:24]:
        copy.wait()

    def prepare_edges(block, carry):
        prepare(block // 4, 0, block % 4, range(8), (0,))
        prepare(block // 4, 3, block % 4, range(8), (1,))
        return carry

    lax.fori_loop(0, 16, prepare_edges, 0)
    for tile_y, halves in ((0, (1,)), (1, (0, 1)), (2, (0, 1)), (3, (0,))):
        prepare(0, tile_y, 0, (0,), halves)
        prepare(3, tile_y, 3, (7,), halves)

    wind_edges = (0, COARSE - 8)
    for b in range(2):
        rows = pl.ds(b * (TILE - 8) + 8, 8)
        for t in range(4):
            lanes = pl.ds(t * TILE, TILE)
            row_send[b, 0:8, lanes] = levels[b * 12 + t, rows, 0:TILE]
            row_send[b, 8:16, lanes] = spreads[b * 12 + t, rows, 0:TILE]
        for c in range(2):
            row_send[b, c * 8 : c * 8 + 8, SIDE : SIDE + 128] = wind[c, pl.ds(wind_edges[b], 8), :]
        for a in range(2):
            diag_send[b * 2 + a, 0:8, :] = levels[b * 12 + a * 3, rows, pl.ds(a * 128, 128)]
            for c in range(2):
                diag_send[b * 2 + a, 8 + c * 8 : 16 + c * 8, :] = wind[c, pl.ds(wind_edges[b], 8), :]
    for a in range(2):
        source = pl.ds(a * 128, 128)
        packed = jnp.zeros((32, 128), F32)
        for g in range(32):
            k = g // 8 * 4 + a * 3
            rows = pl.ds(8 + g % 8 * 32, 32)
            to_level = (4 * g + 2 - (126 if a else 0)) % 128
            to_spread = (4 * g + 1 - (127 if a else 0)) % 128
            moved = jnp.where(
                lane % 4 == 1,
                pltpu.roll(spreads[k, rows, source], to_spread, 1),
                pltpu.roll(levels[k, rows, source], to_level, 1),
            )
            if g < 8:
                to_wind = (4 * g - (127 if a else 0)) % 128
                moved = jnp.where(
                    lane % 4 == 0,
                    pltpu.roll(wind[g // 4, pl.ds((g % 4) * 32, 32), :], to_wind, 1),
                    moved,
                )
            packed = jnp.where(lane // 4 == g, moved, packed)
        col_send[a] = packed

    pl.semaphore_wait(barrier, len(OFFSETS) - 1 + 6)

    halos = []
    for b in range(2):
        halos.append(
            pltpu.make_async_remote_copy(
                src_ref=row_send.at[b], dst_ref=row_recv.at[1 - b],
                send_sem=row_sem.at[b], recv_sem=row_rsem.at[1 - b],
                device_id={"gx": gx_at[b], "gy": gy}, device_id_type=MESH,
            )
        )
        halos.append(
            pltpu.make_async_remote_copy(
                src_ref=col_send.at[b], dst_ref=col_recv.at[1 - b],
                send_sem=col_sem.at[b], recv_sem=col_rsem.at[1 - b],
                device_id={"gx": gx, "gy": gy_at[b]}, device_id_type=MESH,
            )
        )
        for a in range(2):
            k = b * 2 + a
            halos.append(
                pltpu.make_async_remote_copy(
                    src_ref=diag_send.at[k], dst_ref=diag_recv.at[3 - k],
                    send_sem=diag_sem.at[k], recv_sem=diag_rsem.at[3 - k],
                    device_id={"gx": gx_at[b], "gy": gy_at[a]}, device_id_type=MESH,
                )
            )
    for copy in halos:
        copy.start()

    for copy in loads[24:]:
        copy.wait()

    def prepare_rest(block, carry):
        for tile_y, halves in ((0, (1,)), (1, (0, 1)), (2, (0, 1)), (3, (0,))):
            prepare(block // 4, tile_y, block % 4, range(8), halves)
        return carry

    for tile_y, halves in ((0, (1,)), (1, (0, 1)), (2, (0, 1)), (3, (0,))):
        prepare(0, tile_y, 0, range(1, 8), halves)
        prepare(3, tile_y, 3, range(7), halves)
    lax.fori_loop(1, 15, prepare_rest, 0)

    edge_lanes = pl.ds(TILE, 128)

    def set_edges(block, carry):
        rows = pl.ds(pl.multiple_of(block % 4 * 64 + 8, 8), 64)
        k = block // 4 * 4
        for ref in (levels, spreads):
            ref[k, rows, edge_lanes] = ref[k + 1, rows, 0:128]
            for t in (1, 2):
                ref[k + t, rows, edge_lanes] = jnp.where(
                    low_lane, ref[k + t + 1, rows, 0:128], ref[k + t - 1, rows, 128:256]
                )
            ref[k + 3, rows, edge_lanes] = ref[k + 2, rows, 128:256]
        return carry

    lax.fori_loop(0, 16, set_edges, 0)

    for c in range(2):
        wind_pad[c, 8 : 8 + COARSE, 0:128] = wind[c]

    column = lax.broadcasted_iota(jnp.int32, (256, RING), 0)
    column = jnp.where(column >= 192, column - 256, column)
    fire = lax.broadcasted_iota(jnp.int32, (256, RING), 1)
    fire = jnp.where(fire >= 320, fire - RING, fire)
    offset = (fire.astype(F32) + 0.5) * (1.0 / REFINE) - 0.5 - column.astype(F32)

    has_row = (gx > 0, gx < N_GX - 1)
    has_col = (gy > 0, gy < N_GY - 1)

    for copy in halos:
        copy.wait()

    cols = [jnp.where(has_col[a], col_recv[a], 0.0) for a in range(2)]
    for g in range(32):
        rows = pl.ds(8 + g % 8 * 32, 32)
        for ref, item, last in ((levels, 2, 126), (spreads, 1, 127)):
            k = g // 8 * 4
            got = pltpu.roll(cols[0], (last - (4 * g + item)) % 128, 1)
            ref[k, rows, edge_lanes] = jnp.where(low_lane, ref[k, rows, edge_lanes], got)
            got = pltpu.roll(cols[1], (0 - (4 * g + item)) % 128, 1)
            ref[k + 3, rows, edge_lanes] = jnp.where(low_lane, got, ref[k + 3, rows, edge_lanes])
        if g < 8:
            ends = [pltpu.roll(cols[a], ((0 if a else 127) - 4 * g) % 128, 1) for a in range(2)]
            wind_pad[g // 4, pl.ds(8 + (g % 4) * 32, 32), 128:256] = jnp.where(
                low_lane, ends[1], ends[0]
            )
    for b in range(2):
        rows = pl.ds(b * (TILE + 8), 8)
        from_rows = pl.ds(8 if b else TILE, 8)
        for k in range(16):
            if k // 4 == b * 3:
                t = k % 4
                for ref, part in ((levels, 0), (spreads, 8)):
                    got = row_recv[b, part : part + 8, :]
                    ref[k, rows, 0:TILE] = jnp.where(has_row[b], got[:, t * TILE : t * TILE + TILE], 0.0)
                    corner = [
                        jnp.where(has_col[a], diag_recv[b * 2 + a, 0:8, :], 0.0) for a in range(2)
                    ]
                    last = corner[0] if t == 0 else got[:, t * TILE - 128 : t * TILE]
                    after = corner[1] if t == 3 else got[:, t * TILE + TILE : t * TILE + TILE + 128]
                    ref[k, rows, edge_lanes] = jnp.where(
                        has_row[b], jnp.where(low_lane, after, last), 0.0
                    )
            else:
                for ref in (levels, spreads):
                    ref[k, rows, :] = ref[k + (4 if b else -4), from_rows, :]
        wind_at = pl.ds(b * (COARSE + 8), 8)
        for c in range(2):
            wind_pad[c, wind_at, 0:128] = jnp.where(
                has_row[b], row_recv[b, c * 8 : c * 8 + 8, SIDE : SIDE + 128], 0.0
            )
            ends = [
                jnp.where(has_col[a], diag_recv[b * 2 + a, 8 + c * 8 : 16 + c * 8, :], 0.0)
                for a in range(2)
            ]
            wind_pad[c, wind_at, 128:256] = jnp.where(
                has_row[b], jnp.where(low_lane, ends[1], ends[0]), 0.0
            )

    for t in range(4):
        weight = jnp.maximum(1.0 - jnp.abs(offset + 32.0 * t), 0.0).astype(BF16)
        for c in range(2):
            high, low = split(dot2(wind_pad[c], weight))
            for tx in range(4):
                lanes = pl.ds(c * RING, RING)
                winds[tx * 4 + t, 0:48, lanes] = high[tx * 32 : tx * 32 + 48]
                winds[tx * 4 + t, 48:96, lanes] = low[tx * 32 : tx * 32 + 48]

    sub = lax.broadcasted_iota(jnp.int32, (8, RING), 0)
    sub_in = lax.broadcasted_iota(jnp.int32, (8, TILE), 0)
    place = jnp.where(
        lax.broadcasted_iota(jnp.int32, (TILE, 128), 0) // REFINE
        == lax.broadcasted_iota(jnp.int32, (TILE, 128), 1),
        1.0,
        0.0,
    ).astype(BF16)

    def eight(i):
        return pl.ds(pl.multiple_of(i * 8, 8), 8)

    def one_part(n, carry):
        c = n // len(OFFSETS)
        j = n % len(OFFSETS)
        ox = jnp.int32(0)
        oy = jnp.int32(0)
        for i, (dx, dy) in enumerate(OFFSETS):
            now = (j == i).astype(jnp.int32)
            ox = ox + now * dx
            oy = oy + now * dy
        target = ((my_x + ox) % 4) * 4 + (my_y + oy) % 4

        chosen = plan[target]
        part = pl.ds(pl.multiple_of(c * PART, PART), PART)
        fire_wind[...] = jnp.dot(
            row_weight[pl.ds(pl.multiple_of(c * PART, PART), PART + 16), :],
            winds[chosen],
            preferred_element_type=F32,
        )

        def level_rows(i):
            return levels[chosen, eight(c * GROUPS + i), :]

        above = centre = level_rows(0)
        for i in range(GROUPS + 2):
            below = level_rows(i + 1) if i < GROUPS + 1 else centre
            up = pltpu.roll(jnp.where(sub == 7, above, centre), 1, 0)
            down = pltpu.roll(jnp.where(sub == 0, below, centre), 7, 0)
            left = pltpu.roll(centre, 1, 1)
            right = pltpu.roll(centre, RING - 1, 1)
            rows = slice(i * 8, i * 8 + 8)
            halfway[rows, :] = advance(
                centre, up, down, left, right,
                fire_wind[rows, 0:RING], fire_wind[rows, RING : 2 * RING],
                spreads[chosen, eight(c * GROUPS + i), :],
            )
            above, centre = centre, below

        above, centre = halfway[0:8, :], halfway[8:16, :]
        for i in range(GROUPS):
            below = halfway[i * 8 + 16 : i * 8 + 24, :]
            inner = centre[:, 0:TILE]
            up = pltpu.roll(jnp.where(sub_in == 7, above[:, 0:TILE], inner), 1, 0)
            down = pltpu.roll(jnp.where(sub_in == 0, below[:, 0:TILE], inner), 7, 0)
            left = pltpu.roll(centre, 1, 1)[:, 0:TILE]
            right = pltpu.roll(centre, RING - 1, 1)[:, 0:TILE]
            rows = slice(i * 8 + 8, i * 8 + 16)
            padded = eight(c * GROUPS + i + 1)
            result = advance(
                inner, up, down, left, right,
                fire_wind[rows, 0:TILE], fire_wind[rows, RING : RING + TILE],
                spreads[chosen, padded, 0:TILE],
            )
            before = jnp.clip(0.5 - levels[chosen, padded, 0:TILE], 0.0, 1.0)
            after = jnp.clip(0.5 - result, 0.0, 1.0)
            heat = lookup(
                heat_table, 1.0 / (2.0 * TIME_STEP * REFINE * REFINE), fuels[chosen, eight(c * GROUPS + i), :]
            )
            released = heat * (after - before)
            release[0, i * 8 : i * 8 + 8, :] = released[:, 0:128]
            release[1, i * 8 : i * 8 + 8, :] = released[:, 128:256]
            stage[target, eight(c * GROUPS + i), :] = result
            above, centre = centre, below

        @pl.when(j < len(OFFSETS) - 1)
        def _():
            pltpu.make_async_remote_copy(
                src_ref=stage.at[target, part], dst_ref=out.at[gx, part],
                send_sem=send_sem.at[j, c], recv_sem=recv_sem.at[j, c],
                device_id={"gx": target, "gy": gy}, device_id_type=MESH,
            ).start()

        sums = []
        for half in range(2):
            total = release[half, pl.ds(0, GROUPS, stride=8), :]
            for s in range(1, 8):
                total = total + release[half, pl.ds(s, GROUPS, stride=8), :]
            sums.append(total)
        flux[target, pl.ds(pl.multiple_of(c * GROUPS, GROUPS), GROUPS), :] = dot2(
            jnp.concatenate(sums, axis=1), place
        )
        return carry

    lax.fori_loop(0, PARTS * len(OFFSETS), one_part, 0)

    own = pltpu.make_async_copy(stage.at[gx], out.at[gx], own_sem)
    own.start()

    for tx in range(4):
        band = jnp.zeros((32, 128), F32)
        for ty in range(4):
            band = band + pltpu.roll(flux[plan[16 + tx * 4 + ty]], ty * 32, 1)
        for l in range(LEV):
            heating[l, tx * 32 : tx * 32 + 32, :] = profile[l] * band

    own.wait()

    def finish(j, carry):
        for c in range(PARTS):
            part = pl.ds(c * PART, PART)
            pltpu.make_async_remote_copy(
                src_ref=stage.at[gx, part], dst_ref=out.at[gx, part],
                send_sem=send_sem.at[j, c], recv_sem=recv_sem.at[j, c],
                device_id={"gx": (gx + 1) % N_GX, "gy": gy}, device_id_type=MESH,
            ).wait()
        return carry

    lax.fori_loop(0, len(OFFSETS) - 1, finish, 0)


def body(
    level_set, fuel_class, ignition, counts, destination, surface_wind, spread_table, heat_table, profile
):
    hbm = pl.BlockSpec(memory_space=pltpu.HBM)
    vmem = pl.BlockSpec(memory_space=pltpu.VMEM)
    dma = pltpu.SemaphoreType.DMA

    ignition, surface_wind, spread_table, heat_table, destination, profile = (
        pltpu.with_memory_space_constraint(x, pltpu.HBM)
        for x in (ignition, surface_wind, spread_table, heat_table, destination, profile)
    )
    relocated, heating = pl.pallas_call(
        kernel,
        out_shape=(
            jax.ShapeDtypeStruct((N_GX, TILE, TILE), F32),
            jax.ShapeDtypeStruct((LEV, COARSE, COARSE), F32),
        ),
        in_specs=[hbm] * 8,
        out_specs=(vmem, vmem),
        scratch_shapes=[
            pltpu.VMEM((17, TILE + 16, RING), F32),
            pltpu.VMEM((17, TILE + 16, RING), F32),
            pltpu.VMEM((17, TILE, TILE), jnp.int32),
            pltpu.VMEM((17, 96, 2 * RING), BF16),
            pltpu.VMEM((PART + 16, RING), F32),
            pltpu.VMEM((PART + 16, 2 * RING), F32),
            pltpu.VMEM((COARSE, COARSE), jnp.int32),
            pltpu.VMEM((2, COARSE, COARSE), F32),
            pltpu.SMEM((NFUEL,), F32),
            pltpu.SMEM((NFUEL,), F32),
            pltpu.SMEM((4, 4), jnp.int32),
            pltpu.SMEM((LEV,), F32),
            pltpu.SMEM((32,), jnp.int32),
            pltpu.VMEM((2, COARSE + 16, 256), F32),
            pltpu.VMEM((TILE + 16, 96), BF16),
            pltpu.VMEM((4, COARSE, TILE), F32),
            pltpu.VMEM((N_GX, TILE, TILE), F32),
            pltpu.VMEM((2, PART, 128), F32),
            pltpu.VMEM((17, 32, 128), F32),
            pltpu.VMEM((2, 16, SIDE + 128), F32),
            pltpu.VMEM((2, 16, SIDE + 128), F32),
            pltpu.VMEM((2, 32, 128), F32),
            pltpu.VMEM((2, 32, 128), F32),
            pltpu.VMEM((4, 24, 128), F32),
            pltpu.VMEM((4, 24, 128), F32),
            dma((6,)),
            dma((16,)),
            dma((16,)),
            dma((2,)),
            dma((2,)),
            dma((4,)),
            dma((2,)),
            dma((2,)),
            dma((4,)),
            dma((16, PARTS)),
            dma((16, PARTS)),
            dma,
        ],
        compiler_params=pltpu.CompilerParams(
            collective_id=0, has_side_effects=True, vmem_limit_bytes=49 << 20
        ),
    )(
        level_set, fuel_class, ignition, surface_wind, spread_table, heat_table, destination, profile
    )
    return relocated.reshape(1, N_GX, TILE, TILE), heating


def solution(mesh):
    in_specs = (
        P("gx", "gy"),
        P("gx", "gy"),
        P("gx", "gy"),
        P("gx", "gy"),
        P("gx", "gy"),
        P(None, "gx", "gy"),
        P(),
        P(),
        P(),
    )
    out_specs = (P("gy", "gx", None, None), P(None, "gx", "gy"))
    return jax.shard_map(body, mesh=mesh, in_specs=in_specs, out_specs=out_specs, check_vma=False)
```
